128 devices in a mesh: facet: 16 (over z, x_hi, core), vis: 8 (over x_lo, y).
Axes of the slice: x: 4 (x_hi: 2, x_lo: 2; x = x_hi * 2 + x_lo), y: 4, z: 4, core: 2. Of those that a mesh axis runs over, the one named last changes fastest.
Arguments:
- sky_image: float32 [4096, 4096], P('facet', 'vis'), may hold values from -6 to 6
- observed: bfloat16 [128, 256, 256], P(('facet', 'vis')), may hold values from -6 to 6
- offsets: int32 [128, 2], replicated, may hold values from 0 to 4095
- assignments: int32 [128, 8], replicated, may hold values from 0 to 15, all different within a row
Outputs:
- residual_blocks: bfloat16 [128, 256, 256], P(('facet', 'vis'))
- residual_image: float32 [4096, 4096], P('facet', 'vis')
The draws below stay inside these ranges and needn't reach their ends.
Inputs may be any that keep to these rules, and one draw needn't show every extreme that they name: `assignments`: each subgrid names 8 different facets, and every facet is named by some subgrid.
All inputs are finite; a program needn't handle non-finite values.
Results may differ from the reference program's by a relative error of at most 0.017.
Values may be sent and summed in bfloat16 or wider, within the bound.
No kernel may reach another device: no remote copies, remote signals or barrier semaphores. Data moves between devices by JAX's collectives and lax.ppermute only.
A program may use at most 64 MiB of HBM per device.

```python
import jax
import jax.numpy as jnp
from jax import lax

SUB = 256
FW = 4096
FD = 256
FACETS = 16
TOPF = 8
ROWS = 4096
SUBGRIDS = 128


def touch_ends(drawn, stream_key, low, high):
    shape = drawn.shape
    index_at = [jax.random.randint(jax.random.fold_in(stream_key, axis), (), 0, shape[axis]) for axis in range(len(shape))]
    drawn = drawn.at[tuple(index_at)].set(low)
    longest = shape.index(max(shape))
    index_at[longest] = (index_at[longest] + 1) % shape[longest]
    return drawn.at[tuple(index_at)].set(high)


def steps_of(own_key, dims, cuts, smallest, top_value):
    level = 1.0
    for axis_at, shards_of in cuts:
        heights = jax.random.uniform(jax.random.fold_in(jax.random.fold_in(own_key, 6), axis_at), (shards_of,), jnp.float32, smallest / len(cuts), top_value / len(cuts))
        level = level * jnp.repeat(jnp.exp(heights), dims[axis_at] // shards_of).reshape((-1,) + (1,) * (len(dims) - 1 - axis_at))
    return level


def choose_distinct(stream_key, rows, number_of, top, lift):
    order = jax.random.permutation(jax.random.fold_in(stream_key, 1), number_of)
    pull = order
    for power in range(3):
        pull = pull * pull // number_of
    pull = pull * lift // number_of
    lots = jax.random.randint(jax.random.fold_in(stream_key, 2), (rows, number_of), 0, 4096) + pull
    fixed_rows = jax.random.permutation(jax.random.fold_in(stream_key, 3), rows)[jnp.arange(number_of) % rows]
    lots = jnp.where(jnp.arange(rows)[:, None] == fixed_rows[None, :], 1 << 14, lots)
    merit = lots * number_of + jnp.arange(number_of)
    return lax.top_k(merit.astype(jnp.int32), top)[1].astype(jnp.int32)


def bell_draw(own_key, extent, scale, reach, shards=(), kind=jnp.bfloat16):
    level = steps_of(own_key, extent, shards, -0.22, 0.18) if shards else 1.0
    array = jax.random.normal(own_key, extent, jnp.float32) * scale * level
    return jnp.minimum(jnp.maximum(array, -reach), reach).astype(kind)


def setup_inputs(seed: int = 0) -> dict:
    seeds = jax.random.split(jax.random.key(seed), 5)
    sky_image = bell_draw(seeds[0], (ROWS, FW), 1.0, 6.0, ((0, 16), (1, 8)), jnp.float32)
    observed = bell_draw(seeds[1], (SUBGRIDS, SUB, SUB), 1.0, 6.0, ((0, 128),))
    offsets = touch_ends(jax.random.randint(seeds[2], (SUBGRIDS, 2), 0, FW), jax.random.fold_in(seeds[2], 1), 0, FW - 1).astype(jnp.int32)
    assignments = choose_distinct(seeds[3], SUBGRIDS, FACETS, TOPF, 8192)
    return dict(sky_image=sky_image, observed=observed, offsets=offsets, assignments=assignments)


def cas_table(freqs, places, period, factor):
    phase = (freqs[:, None] % period) * places[None, :] % period
    angle = phase.astype(jnp.float32) * (2.0 * jnp.pi / period)
    return ((jnp.cos(angle) + jnp.sin(angle)) * factor).astype(jnp.bfloat16)


def reference(sky_image, observed, offsets, assignments):
    all_rows = FD * FACETS
    hp = lax.Precision.HIGHEST
    model_b = sky_image.astype(jnp.bfloat16).astype(jnp.float32)
    col_ids = jnp.arange(FW, dtype=jnp.int32)
    row_ids = jnp.arange(all_rows, dtype=jnp.int32)
    sub_ids = jnp.arange(SUB, dtype=jnp.int32)
    pred_table = cas_table(col_ids, col_ids, FW, FW ** -0.5).astype(jnp.float32)
    spectrum = jnp.dot(model_b, pred_table.T, precision=hp)
    facet_of_row = row_ids // FD

    def per_subgrid(acc_grid, sub_index):
        col_freq = (offsets[sub_index, 0] + sub_ids) % FW
        row_freq = offsets[sub_index, 1] + sub_ids
        inner = jnp.take(spectrum, col_freq, axis=1).astype(jnp.bfloat16).astype(jnp.float32)
        row_pred = cas_table(row_freq, row_ids, all_rows, all_rows ** -0.5).astype(jnp.float32)
        predicted = jnp.dot(row_pred, inner, precision=hp)
        resid = (observed[sub_index].astype(jnp.float32) - predicted).astype(jnp.bfloat16)
        row_grid = cas_table(row_freq, row_ids, all_rows, SUB ** -0.5).astype(jnp.float32)
        left = jnp.dot(row_grid.T, resid.astype(jnp.float32), precision=hp).astype(jnp.bfloat16)
        keep = jnp.any(assignments[sub_index][:, None] == facet_of_row[None, :], axis=0)
        left = jnp.where(keep[:, None], left.astype(jnp.float32), jnp.float32(0.0))
        acc_grid = acc_grid.at[:, col_freq].add(left)
        return acc_grid, resid

    start_grid = jnp.zeros((all_rows, FW), jnp.float32)
    freq_grid, blocks_out = lax.scan(per_subgrid, start_grid, jnp.arange(SUBGRIDS, dtype=jnp.int32))
    grid_table = cas_table(col_ids, col_ids, FW, SUB ** -0.5).astype(jnp.float32)
    image_out = jnp.dot(freq_grid, grid_table, precision=hp)
    return blocks_out, image_out
```

```python
import jax
import jax.numpy as jnp
import ml_dtypes
import numpy as np
from jax import lax
from jax.experimental import pallas as pl
from jax.experimental.pallas import tpu as pltpu
from jax.sharding import PartitionSpec as P

F32 = jnp.float32
BF16 = jnp.bfloat16
N = 4096
SUB = 256
HALF = 0.5**0.5
NT = (((1,), (1,)), ((), ()))


def turn(phase, period):
    angle = (2.0 * np.pi / period) * (phase % period)
    return np.cos(angle), np.sin(angle)


def bf(table):
    return table.astype(ml_dtypes.bfloat16)


def column_tables():
    order = np.arange(512)
    k1 = 16 * (order % 32) + order // 32
    c, s = turn(np.arange(512)[:, None] * k1[None, :], 512)
    ahead = bf(np.concatenate([c + s, c - s], axis=0) / 64.0)
    back = bf(np.concatenate([c.T, s.T], axis=1) / 16.0)
    c, s = turn(np.arange(8)[:, None] * np.arange(512)[None, :], N)
    return ahead, back, np.concatenate([c, s], axis=0).astype(np.float32)


def row_table():
    g = np.arange(N).reshape(16, 256)
    c, s = turn(g[:, :, None] * np.arange(SUB)[None, None, :], N)
    return bf(np.stack([c + s, c - s], axis=1).reshape(2 * N, SUB))


def own_index():
    return lax.axis_index("facet") * 8 + lax.axis_index("vis")


def lane_group(rows):
    return lax.broadcasted_iota(jnp.int32, (rows, 128), 1) >> 5


def swap_groups(parts, group):
    out = []
    for j in range(4):
        moved = [pltpu.roll(parts[i], (32 * (i - j)) % 128, 1) if i != j else parts[i] for i in range(4)]
        mixed = jnp.where(group < 2, jnp.where(group == 0, moved[0], moved[1]), jnp.where(group == 2, moved[2], moved[3]))
        out.append(mixed)
    return out


def block_selector(u):
    row = lax.broadcasted_iota(jnp.int32, (1024, 512), 0)
    col = lax.broadcasted_iota(jnp.int32, (1024, 512), 1)
    hit = ((row & 7) == (col >> 7)) & ((((row >> 3) - u) & 127) == (col & 127))
    return jnp.where(hit, 1.0, 0.0).astype(BF16)


def columns_ahead(rx_ref, obs_ref, off_ref, tw_ref, tab_ref, out_ref):
    x = [rx_ref[j].astype(F32) for j in range(8)]
    e = [x[i] + x[i + 4] for i in range(4)]
    o = [x[i] - x[i + 4] for i in range(4)]
    up, down = (o[1] + o[3]) * HALF, (o[1] - o[3]) * HALF
    e02, e13 = e[0] + e[2], e[1] + e[3]
    d1 = (o[0] + down, o[2] + up)
    d2 = (e[0] - e[2], e[1] - e[3])
    d3 = (o[0] - down, up - o[2])
    spec = [(e02 + e13, None), d1, d2, d3, (e02 - e13, None), (d3[0], -d3[1]), (d2[0], -d2[1]), (d1[0], -d1[1])]
    rows = []
    for k2 in range(8):
        c, s = tw_ref[k2 : k2 + 1, :], tw_ref[8 + k2 : 9 + k2, :]
        re, im = spec[k2]
        if im is None:
            zr, zi = re * c, re * s
        else:
            zr, zi = re * c - im * s, re * s + im * c
        rows.append(jnp.concatenate([zr, zi], axis=1))
    left = jnp.concatenate(rows, axis=0).astype(BF16)
    freq = jnp.dot(left, tab_ref[...], preferred_element_type=F32)

    u = off_ref[own_index(), 0]
    obs = obs_ref[0]
    quarters = jnp.concatenate([obs[:128, :128], obs[128:, :128], obs[:128, 128:], obs[128:, 128:]], axis=1)
    seen = lax.dot_general(block_selector(u), quarters, NT, preferred_element_type=F32).reshape(128, 8, 128)

    group = lane_group(64)
    for qg in range(4):
        part = freq[:, 128 * qg : 128 * qg + 128].reshape(8, 4, 8, 128)
        tiles = swap_groups([part[:, rg].reshape(64, 128) for rg in range(4)], group)
        for q4 in range(4):
            at = 8 * (4 * qg + q4)
            block = jnp.concatenate([tiles[q4].reshape(8, 8, 128), seen[at : at + 8]], axis=1)
            out_ref[at : at + 8] = block.astype(BF16)


def spin(re, im, c, s):
    return re * c - im * s, re * s + im * c


def cos_sin(phase):
    angle = (phase & (N - 1)).astype(F32) * np.float32(2.0 * np.pi / N)
    return jnp.cos(angle), jnp.sin(angle)


def rows_kernel(rx_ref, off_ref, asg_ref, tab_ref, out_ref, ybuf, ec, es, ect, est, rr):
    me = own_index()
    off = off_ref[...]
    u, v = off[:, 0:1], off[:, 1:2]
    first = (me - u) & 127
    s0 = ((u + first - me) >> 7) & 31
    lane = lax.broadcasted_iota(jnp.int32, (128, 128), 1)
    chosen0 = jnp.where((lane & 31) == s0, 1.0, 0.0)
    chosen1 = jnp.where((lane & 31) == ((s0 + 1) & 31), 1.0, 0.0)
    chosen = jnp.concatenate([chosen0, chosen1], axis=0).astype(BF16)

    v_row = jnp.transpose(jnp.broadcast_to(v.astype(F32), (128, 128)))[:16].astype(jnp.int32)
    step = lax.broadcasted_iota(jnp.int32, (16, 128), 0)
    lo_c, lo_s = cos_sin(v_row * step)
    hi_c, hi_s = cos_sin(v_row * step * 16)
    pairs = [spin(lo_c, lo_s, hi_c[i : i + 1], hi_s[i : i + 1]) for i in range(16)]
    base_c = jnp.concatenate([p[0] for p in pairs], axis=0)
    base_s = jnp.concatenate([p[1] for p in pairs], axis=0)
    ec[...], es[...] = base_c, base_s
    ect[...], est[...] = jnp.transpose(base_c), jnp.transpose(base_s)
    turn_c, turn_s = cos_sin(v_row[:8] * 256)
    turn_ct = jnp.transpose(jnp.broadcast_to(turn_c[:1], (256, 128)))
    turn_st = jnp.transpose(jnp.broadcast_to(turn_s[:1], (256, 128)))
    group = lax.broadcasted_iota(jnp.int32, (8, 8, 128), 2) >> 5

    @pl.loop(0, 16)
    def _(f):
        tile = rx_ref[pl.ds(8 * f, 8)].astype(F32)[:, 0:8]
        spread = jnp.stack([jnp.where(group == rg, tile, 0.0) for rg in range(4)], axis=1)
        right = spread.reshape(256, 128).astype(BF16)
        cols = lax.dot_general(chosen, right, NT, preferred_element_type=F32)
        c, s = ect[...], est[...]
        at = pl.multiple_of(f * 512, 512)
        for t in range(2):
            half = cols[128 * t : 128 * t + 128]
            ybuf[128 * t : 128 * t + 128, pl.ds(at, 256)] = (half * c).astype(BF16)
            ybuf[128 * t : 128 * t + 128, pl.ds(at + 256, 256)] = (half * s).astype(BF16)
        ect[...], est[...] = spin(c, s, turn_ct, turn_st)

    pred = jnp.dot(ybuf[...], tab_ref[...], preferred_element_type=F32) * (1.0 / 64.0)

    seen = rx_ref[...].astype(F32)[:, 8:16].reshape(1024, 128).astype(BF16)
    row = lax.broadcasted_iota(jnp.int32, (256, 1024), 0)
    col = lax.broadcasted_iota(jnp.int32, (256, 1024), 1)
    same = (col >> 3) == (row & 127)
    obs = []
    for ah in range(2):
        pick = jnp.where(same & ((col & 7) == 2 * (row >> 7) + ah), 1.0, 0.0).astype(BF16)
        obs.append(jnp.dot(pick, seen, preferred_element_type=F32))
    resid = (jnp.concatenate(obs, axis=1) - pred).astype(BF16)
    row = lax.broadcasted_iota(jnp.int32, (1024, 256), 0)
    col = lax.broadcasted_iota(jnp.int32, (1024, 256), 1)
    same = (row >> 3) == (col & 127)
    back = jnp.zeros((1024, 128), F32)
    for ah in range(2):
        pick = jnp.where(same & ((row & 7) == 2 * (col >> 7) + ah), 1.0, 0.0).astype(BF16)
        back = back + jnp.dot(pick, resid[:, 128 * ah : 128 * ah + 128], preferred_element_type=F32)
    rr[...] = back.reshape(128, 8, 128)

    bits = jnp.sum(lax.shift_left(jnp.ones_like(asg_ref[...]), asg_ref[...]).astype(F32), axis=1, keepdims=True)
    bits = jnp.broadcast_to(bits, (128, 128)).astype(jnp.int32)

    @pl.loop(0, 16)
    def _(f):
        at = pl.multiple_of(f * 512, 512)
        w1 = lax.dot_general(tab_ref[pl.ds(at, 256), :], resid, NT, preferred_element_type=F32)
        w2 = lax.dot_general(tab_ref[pl.ds(at + 256, 256), :], resid, NT, preferred_element_type=F32)
        c, s = ec[...], es[...]
        z = [c * w1[:, 128 * t : 128 * t + 128] + s * w2[:, 128 * t : 128 * t + 128] for t in range(2)]
        z = jnp.concatenate(z, axis=1).astype(BF16)
        named = (lax.shift_right_logical(bits, f) & 1) == 1
        keep = jnp.concatenate([jnp.where(named, chosen0, 0.0), jnp.where(named, chosen1, 0.0)], axis=0).astype(BF16)
        grid = jnp.dot(z, keep, preferred_element_type=F32).reshape(8, 4, 8, 128)
        mixed = jnp.where(
            group < 2,
            jnp.where(group == 0, grid[:, 0], grid[:, 1]),
            jnp.where(group == 2, grid[:, 2], grid[:, 3]),
        )
        block = jnp.concatenate([mixed * (1.0 / 16.0), rr[pl.ds(8 * f, 8)]], axis=1)
        out_ref[pl.ds(8 * f, 8)] = block.astype(BF16)
        nc, ns = spin(c.reshape(32, 8, 128), s.reshape(32, 8, 128), turn_c[None], turn_s[None])
        ec[...], es[...] = nc.reshape(256, 128), ns.reshape(256, 128)


def columns_back(rx_ref, off_ref, tw_ref, tab_ref, img_ref, res_ref):
    got = rx_ref[...].astype(F32)
    tiles = got[:, 0:8].reshape(16, 64, 128)
    group = lane_group(64)
    wide = [[None] * 4 for _ in range(4)]
    for qg in range(4):
        mixed = swap_groups([tiles[4 * qg + q4] for q4 in range(4)], group)
        for rg in range(4):
            wide[rg][qg] = mixed[rg].reshape(8, 8, 128)
    left = jnp.stack([jnp.concatenate(wide[rg], axis=2) for rg in range(4)], axis=1)
    left = left.reshape(256, 512).astype(BF16)
    both = jnp.dot(left, tab_ref[...], preferred_element_type=F32).reshape(8, 32, 1024)
    re, im = [], []
    for k2 in range(8):
        c, s = tw_ref[k2 : k2 + 1, :], tw_ref[8 + k2 : 9 + k2, :]
        a, b = spin(both[k2, :, :512], both[k2, :, 512:], c + s, s - c)
        re.append(a)
        im.append(b)
    a1, a2, a3 = re[1] + re[7], re[2] + re[6], re[3] + re[5]
    b1, b2, b3 = im[1] - im[7], im[2] - im[6], im[3] - im[5]
    plus, minus = re[0] + re[4], re[0] - re[4]
    even = [plus + a2, minus - b2, plus - a2, minus + b2]
    odd = [a1 + a3, HALF * (a1 - b1 - a3 - b3), b3 - b1, HALF * (a3 - a1 - b1 - b3)]
    for j in range(4):
        img_ref[j] = (even[j] + odd[j]).astype(BF16)
        img_ref[j + 4] = (even[j] - odd[j]).astype(BF16)

    u = off_ref[own_index(), 0]
    back = jnp.transpose(got[:, 8:16].reshape(1024, 128)).astype(BF16)
    quarters = jnp.dot(back, block_selector(u), preferred_element_type=F32).astype(BF16)
    for t in range(2):
        for ah in range(2):
            i = 2 * t + ah
            res_ref[0, 128 * ah : 128 * ah + 128, 128 * t : 128 * t + 128] = quarters[:, 128 * i : 128 * i + 128]


VMEM = pl.BlockSpec(memory_space=pltpu.VMEM)
SMEM = pl.BlockSpec(memory_space=pltpu.SMEM)
PARAMS = pltpu.CompilerParams(vmem_limit_bytes=56 * 2**20)


def on_device(sky_image, observed, offsets, assignments):
    ahead, back, twiddle = column_tables()
    rows = row_table()
    everyone = ("facet", "vis")
    message = jax.ShapeDtypeStruct((128, 16, 128), BF16)

    strips = sky_image.astype(BF16).reshape(8, 32, 512)
    strips = lax.all_to_all(strips, "vis", 0, 0, tiled=True)
    sent = pl.pallas_call(
        columns_ahead,
        out_shape=message,
        in_specs=[VMEM, VMEM, SMEM, VMEM, VMEM],
        out_specs=VMEM,
        compiler_params=PARAMS,
    )(strips, observed, offsets, jnp.asarray(twiddle), jnp.asarray(ahead))
    got = lax.all_to_all(sent, everyone, 0, 0, tiled=True)
    sent = pl.pallas_call(
        rows_kernel,
        out_shape=message,
        in_specs=[VMEM, VMEM, VMEM, VMEM],
        out_specs=VMEM,
        scratch_shapes=[
            pltpu.VMEM((256, 2 * N), BF16),
            pltpu.VMEM((256, 128), F32),
            pltpu.VMEM((256, 128), F32),
            pltpu.VMEM((128, 256), F32),
            pltpu.VMEM((128, 256), F32),
            pltpu.VMEM((128, 8, 128), F32),
        ],
        compiler_params=PARAMS,
    )(got, offsets, assignments, jnp.asarray(rows))
    got = lax.all_to_all(sent, everyone, 0, 0, tiled=True)
    image, resid = pl.pallas_call(
        columns_back,
        out_shape=(
            jax.ShapeDtypeStruct((8, 32, 512), BF16),
            jax.ShapeDtypeStruct((1, SUB, SUB), BF16),
        ),
        in_specs=[VMEM, SMEM, VMEM, VMEM],
        out_specs=(VMEM, VMEM),
        compiler_params=PARAMS,
    )(got, offsets, jnp.asarray(twiddle), jnp.asarray(back))
    image = lax.all_to_all(image, "vis", 0, 0, tiled=True)
    return resid, image.reshape(256, 512).astype(F32)


def solution(mesh):
    placed = (P("facet", "vis"), P(("facet", "vis"), None, None), P(), P())
    return jax.shard_map(
        on_device,
        mesh=mesh,
        in_specs=placed,
        out_specs=(P(("facet", "vis"), None, None), P("facet", "vis")),
        check_vma=False,
    )
```

```python
import jax
import jax.numpy as jnp
import ml_dtypes
import numpy as np
from jax import lax
from jax.experimental import pallas as pl
from jax.experimental.pallas import tpu as pltpu
from jax.sharding import PartitionSpec as P

F32 = jnp.float32
BF16 = jnp.bfloat16
N = 4096
SUB = 256
HALF = 0.5**0.5
NT = (((1,), (1,)), ((), ()))


def turn(phase, period):
    angle = (2.0 * np.pi / period) * (phase % period)
    return np.cos(angle), np.sin(angle)


def bf(table):
    return table.astype(ml_dtypes.bfloat16)


def column_tables():
    order = np.arange(512)
    k1 = 16 * (order % 32) + order // 32
    c, s = turn(np.arange(512)[:, None] * k1[None, :], 512)
    ahead = bf(np.concatenate([c + s, c - s], axis=0) / 64.0)
    back = bf(np.concatenate([c.T, s.T], axis=1) / 16.0)
    c, s = turn(np.arange(8)[:, None] * np.arange(512)[None, :], N)
    return ahead, back, np.concatenate([c, s], axis=0).astype(np.float32)


def row_table():
    g = np.arange(N).reshape(16, 256)
    c, s = turn(g[:, :, None] * np.arange(SUB)[None, None, :], N)
    return bf(np.stack([c + s, c - s], axis=1).reshape(2 * N, SUB))


def own_index():
    return lax.axis_index("facet") * 8 + lax.axis_index("vis")


def lane_group(rows):
    return lax.broadcasted_iota(jnp.int32, (rows, 128), 1) >> 5


def swap_groups(parts, group):
    out = []
    for j in range(4):
        moved = [pltpu.roll(parts[i], (32 * (i - j)) % 128, 1) if i != j else parts[i] for i in range(4)]
        mixed = jnp.where(group < 2, jnp.where(group == 0, moved[0], moved[1]), jnp.where(group == 2, moved[2], moved[3]))
        out.append(mixed)
    return out


def block_selector(u):
    row = lax.broadcasted_iota(jnp.int32, (1024, 512), 0)
    col = lax.broadcasted_iota(jnp.int32, (1024, 512), 1)
    hit = ((row & 7) == (col >> 7)) & ((((row >> 3) - u) & 127) == (col & 127))
    return jnp.where(hit, 1.0, 0.0).astype(BF16)


def spin(re, im, c, s):
    return re * c - im * s, re * s + im * c


def cos_sin(phase):
    angle = (phase & (N - 1)).astype(F32) * np.float32(2.0 * np.pi / N)
    return jnp.cos(angle), jnp.sin(angle)


def tables(off_ref, asg_ref, ct_ref, st_ref, cg_ref, sg_ref, tc_ref, ts_ref, chosen_ref, bits_ref):
    me = own_index()
    v_row = jnp.broadcast_to(off_ref[1:2, :], (16, 128))
    step = lax.broadcasted_iota(jnp.int32, (16, 128), 0)
    lo_c, lo_s = cos_sin(v_row * step)
    hi_c, hi_s = cos_sin(v_row * step * 16)
    top_c, top_s = cos_sin(v_row * 256)
    pairs = [spin(lo_c, lo_s, hi_c[i : i + 1], hi_s[i : i + 1]) for i in range(16)]
    c = jnp.concatenate([p[0] for p in pairs], axis=0)
    s = jnp.concatenate([p[1] for p in pairs], axis=0)
    cg_ref[...], sg_ref[...] = c, s
    ct_ref[...], st_ref[...] = jnp.transpose(c), jnp.transpose(s)
    tc_ref[...], ts_ref[...] = top_c, top_s

    u = off_ref[0:1, :]
    first = (me - u) & 127
    s0 = ((u + first - me) >> 7) & 31
    lane = lax.broadcasted_iota(jnp.int32, (128, 128), 0) & 31
    for t in range(2):
        hit = jnp.where(lane == ((s0 + t) & 31), 1.0, 0.0)
        chosen_ref[128 * t : 128 * t + 128] = jnp.transpose(hit)
    asg = asg_ref[...]
    bits = jnp.sum(lax.shift_left(jnp.ones_like(asg), asg).astype(F32), axis=0, keepdims=True)
    bits_ref[...] = jnp.transpose(jnp.broadcast_to(bits, (128, 128))).astype(jnp.int32)


def round_image(sky_hbm, out_ref, held, sems):
    moves = [pltpu.make_async_copy(sky_hbm.at[pl.ds(64 * i, 64)], held.at[pl.ds(64 * i, 64)], sems.at[i]) for i in range(4)]
    for move in moves:
        move.start()
    for i, move in enumerate(moves):
        move.wait()
        out_ref[2 * i : 2 * i + 2] = held[64 * i : 64 * i + 64].reshape(2, 32, 512).astype(BF16)


def columns_ahead(rx_ref, obs_hbm, off_ref, big_hbm, out_ref, obs_ref, tab_ref, sems):
    moves = [pltpu.make_async_copy(obs_hbm, obs_ref, sems.at[0])]
    for i in range(2):
        half = big_hbm.at[pl.ds(2 * N + 1024 * i, 1024)]
        moves.append(pltpu.make_async_copy(half, tab_ref.at[:, pl.ds(256 * i, 256)], sems.at[1 + i]))
    for move in moves:
        move.start()
    k2 = lax.broadcasted_iota(jnp.int32, (8, 512), 0)
    twist_c, twist_s = cos_sin(k2 * lax.broadcasted_iota(jnp.int32, (8, 512), 1))
    x = [rx_ref[j].astype(F32) for j in range(8)]
    e = [x[i] + x[i + 4] for i in range(4)]
    o = [x[i] - x[i + 4] for i in range(4)]
    up, down = (o[1] + o[3]) * HALF, (o[1] - o[3]) * HALF
    e02, e13 = e[0] + e[2], e[1] + e[3]
    d1 = (o[0] + down, o[2] + up)
    d2 = (e[0] - e[2], e[1] - e[3])
    d3 = (o[0] - down, up - o[2])
    spec = [(e02 + e13, None), d1, d2, d3, (e02 - e13, None), (d3[0], -d3[1]), (d2[0], -d2[1]), (d1[0], -d1[1])]
    rows = []
    for k2 in range(8):
        c, s = twist_c[k2 : k2 + 1], twist_s[k2 : k2 + 1]
        re, im = spec[k2]
        if im is None:
            zr, zi = re * c, re * s
        else:
            zr, zi = re * c - im * s, re * s + im * c
        rows.append(jnp.concatenate([zr, zi], axis=1))
    left = jnp.concatenate(rows, axis=0).astype(BF16)
    for move in moves:
        move.wait()
    freq = jnp.dot(left, tab_ref[...], preferred_element_type=F32)

    u = off_ref[0:1, :]
    place = lax.broadcasted_iota(jnp.int32, (1, 128), 1)
    u = jnp.sum(jnp.where(place == own_index(), u, 0).astype(F32), axis=1, keepdims=True).astype(jnp.int32)
    obs = obs_ref[0]
    quarters = jnp.concatenate([obs[:128, :128], obs[128:, :128], obs[:128, 128:], obs[128:, 128:]], axis=1)
    seen = lax.dot_general(block_selector(u), quarters, NT, preferred_element_type=F32).reshape(128, 8, 128)

    group = lane_group(64)
    for qg in range(4):
        part = freq[:, 128 * qg : 128 * qg + 128].reshape(8, 4, 8, 128)
        tiles = swap_groups([part[:, rg].reshape(64, 128) for rg in range(4)], group)
        for q4 in range(4):
            at = 8 * (4 * qg + q4)
            tile = tiles[q4].reshape(8, 8, 128).astype(BF16)
            out_ref[at : at + 8, 0] = tile[:, 0:4]
            out_ref[at : at + 8, 1] = tile[:, 4:8]
            out_ref[at : at + 8, 2] = seen[at : at + 8, 0:4].astype(BF16)


def rows_kernel(
    rx_ref, off_ref, asg_ref, big_hbm,
    out_ref, ybuf, held, obs, rr, ct, st, cg, sg, tc_ref, ts_ref, chosen_ref, bits_ref, tab_ref, sem,
):
    fetch = pltpu.make_async_copy(big_hbm.at[pl.ds(0, 2 * N)], tab_ref, sem)
    fetch.start()
    tables(off_ref, asg_ref, ct, st, cg, sg, tc_ref, ts_ref, chosen_ref, bits_ref)
    group = lax.broadcasted_iota(jnp.int32, (8, 8, 128), 2) >> 5
    got = rx_ref[...].astype(F32)
    held[:, 0:4] = got[:, 0]
    held[:, 4:8] = got[:, 1]
    obs[:, 0:4] = got[:, 2]
    chosen = chosen_ref[...].astype(BF16)
    turn_ct = jnp.transpose(jnp.broadcast_to(tc_ref[:1], (256, 128)))
    turn_st = jnp.transpose(jnp.broadcast_to(ts_ref[:1], (256, 128)))

    @pl.loop(0, 16, unroll=UNROLL)
    def _(f):
        tile = held[pl.ds(8 * f, 8)]
        spread = jnp.stack([jnp.where(group == rg, tile, 0.0) for rg in range(4)], axis=1)
        right = spread.reshape(256, 128).astype(BF16)
        cols = lax.dot_general(chosen, right, NT, preferred_element_type=F32)
        at = pl.multiple_of(f * 512, 512)
        c, s = ct[...], st[...]
        for t in range(2):
            half = cols[128 * t : 128 * t + 128]
            ybuf[128 * t : 128 * t + 128, pl.ds(at, 256)] = (half * c).astype(BF16)
            ybuf[128 * t : 128 * t + 128, pl.ds(at + 256, 256)] = (half * s).astype(BF16)
        ct[...], st[...] = spin(c, s, turn_ct, turn_st)

    fetch.wait()
    pred = jnp.dot(ybuf[...], tab_ref[...], preferred_element_type=F32) * (1.0 / 64.0)
    resid = []
    seen, back = obs.reshape(1024, 128), rr.reshape(1024, 128)
    for t in range(2):
        halves = []
        for ah in range(2):
            quarter = seen[pl.ds(2 * t + ah, 128, stride=8), :] - pred[128 * t : 128 * t + 128, 128 * ah : 128 * ah + 128]
            halves.append(quarter.astype(BF16))
            back[pl.ds(2 * t + ah, 128, stride=8), :] = quarter
        resid.append(jnp.concatenate(halves, axis=1))
    resid = jnp.concatenate(resid, axis=0)
    turn_c, turn_s = tc_ref[:8][None], ts_ref[:8][None]

    @pl.loop(0, 16, unroll=UNROLL)
    def _(f):
        at = pl.multiple_of(f * 512, 512)
        both = lax.dot_general(tab_ref[pl.ds(at, 512), :], resid, NT, preferred_element_type=F32)
        w1, w2 = both[:256], both[256:]
        c, s = cg[...], sg[...]
        z = [c * w1[:, 128 * t : 128 * t + 128] + s * w2[:, 128 * t : 128 * t + 128] for t in range(2)]
        z = jnp.concatenate(z, axis=1).astype(BF16)
        named = (lax.shift_right_logical(bits_ref[...], f) & 1) == 1
        keep = [jnp.where(named, chosen_ref[128 * t : 128 * t + 128], 0.0) for t in range(2)]
        keep = jnp.concatenate(keep, axis=0).astype(BF16)
        grid = jnp.dot(z, keep, preferred_element_type=F32).reshape(8, 4, 8, 128)
        mixed = jnp.where(
            group < 2,
            jnp.where(group == 0, grid[:, 0], grid[:, 1]),
            jnp.where(group == 2, grid[:, 2], grid[:, 3]),
        )
        mixed = (mixed * (1.0 / 16.0)).astype(BF16)
        out_ref[pl.ds(8 * f, 8), 0] = mixed[:, 0:4]
        out_ref[pl.ds(8 * f, 8), 1] = mixed[:, 4:8]
        out_ref[pl.ds(8 * f, 8), 2] = rr[pl.ds(8 * f, 8)][:, 0:4].astype(BF16)
        nc, ns = spin(c.reshape(32, 8, 128), s.reshape(32, 8, 128), turn_c, turn_s)
        cg[...], sg[...] = nc.reshape(256, 128), ns.reshape(256, 128)


def columns_back(rx_ref, off_ref, tw_ref, tab_ref, img_ref, res_ref, held, sent):
    got = rx_ref[...].astype(F32)
    held[:, 0:4] = got[:, 0]
    held[:, 4:8] = got[:, 1]
    tiles = held[...].reshape(16, 64, 128)
    group = lane_group(64)
    wide = [[None] * 4 for _ in range(4)]
    for qg in range(4):
        mixed = swap_groups([tiles[4 * qg + q4] for q4 in range(4)], group)
        for rg in range(4):
            wide[rg][qg] = mixed[rg].reshape(8, 8, 128)
    left = jnp.stack([jnp.concatenate(wide[rg], axis=2) for rg in range(4)], axis=1)
    left = left.reshape(256, 512).astype(BF16)
    both = jnp.dot(left, tab_ref[...], preferred_element_type=F32).reshape(8, 32, 1024)
    re, im = [], []
    for k2 in range(8):
        c, s = tw_ref[k2 : k2 + 1, :], tw_ref[8 + k2 : 9 + k2, :]
        a, b = spin(both[k2, :, :512], both[k2, :, 512:], c + s, s - c)
        re.append(a)
        im.append(b)
    a1, a2, a3 = re[1] + re[7], re[2] + re[6], re[3] + re[5]
    b1, b2, b3 = im[1] - im[7], im[2] - im[6], im[3] - im[5]
    plus, minus = re[0] + re[4], re[0] - re[4]
    even = [plus + a2, minus - b2, plus - a2, minus + b2]
    odd = [a1 + a3, HALF * (a1 - b1 - a3 - b3), b3 - b1, HALF * (a3 - a1 - b1 - b3)]
    for j in range(4):
        img_ref[j] = (even[j] + odd[j]).astype(BF16)
        img_ref[j + 4] = (even[j] - odd[j]).astype(BF16)

    u = off_ref[0, own_index()]
    sent[...] = jnp.zeros_like(sent)
    sent[:, 0:4] = got[:, 2]
    back = jnp.transpose(sent[...].reshape(1024, 128)).astype(BF16)
    quarters = jnp.dot(back, block_selector(u), preferred_element_type=F32).astype(BF16)
    for t in range(2):
        for ah in range(2):
            i = 2 * t + ah
            res_ref[0, 128 * ah : 128 * ah + 128, 128 * t : 128 * t + 128] = quarters[:, 128 * i : 128 * i + 128]


VMEM = pl.BlockSpec(memory_space=pltpu.VMEM)
SMEM = pl.BlockSpec(memory_space=pltpu.SMEM)
HBM = pl.BlockSpec(memory_space=pltpu.HBM)
UNROLL = 4
L0, L1, L2 = 53, 53, 53


def params(mebibytes):
    return pltpu.CompilerParams(vmem_limit_bytes=mebibytes * 2**20)


def on_device(sky_image, observed, offsets, assignments):
    ahead, back, twiddle = column_tables()
    big = jnp.asarray(np.concatenate([row_table(), ahead[:, :256], ahead[:, 256:]], axis=0))
    everyone = ("facet", "vis")
    message = jax.ShapeDtypeStruct((128, 3, 4, 128), BF16)
    offsets, assignments = offsets.T, assignments.T

    strips = pl.pallas_call(
        round_image,
        out_shape=jax.ShapeDtypeStruct((8, 32, 512), BF16),
        in_specs=[HBM],
        out_specs=VMEM,
        scratch_shapes=[pltpu.VMEM((256, 512), F32), pltpu.SemaphoreType.DMA((4,))],
        compiler_params=params(L0),
    )(sky_image)
    strips = lax.all_to_all(strips, "vis", 0, 0, tiled=True)
    sent = pl.pallas_call(
        columns_ahead,
        out_shape=message,
        in_specs=[VMEM, HBM, VMEM, HBM],
        out_specs=VMEM,
        scratch_shapes=[
            pltpu.VMEM((1, SUB, SUB), BF16),
            pltpu.VMEM((1024, 512), BF16),
            pltpu.SemaphoreType.DMA((3,)),
        ],
        compiler_params=params(L1),
    )(strips, observed, offsets, big)
    got = lax.all_to_all(sent, everyone, 0, 0, tiled=True)
    sent = pl.pallas_call(
        rows_kernel,
        out_shape=message,
        in_specs=[VMEM, VMEM, VMEM, HBM],
        out_specs=VMEM,
        scratch_shapes=[
            pltpu.VMEM((256, 2 * N), BF16),
            pltpu.VMEM((128, 8, 128), F32),
            pltpu.VMEM((128, 8, 128), F32),
            pltpu.VMEM((128, 8, 128), F32),
            pltpu.VMEM((128, 256), F32),
            pltpu.VMEM((128, 256), F32),
            pltpu.VMEM((256, 128), F32),
            pltpu.VMEM((256, 128), F32),
            pltpu.VMEM((16, 128), F32),
            pltpu.VMEM((16, 128), F32),
            pltpu.VMEM((256, 128), F32),
            pltpu.VMEM((128, 128), jnp.int32),
            pltpu.VMEM((2 * N, 256), BF16),
            pltpu.SemaphoreType.DMA,
        ],
        compiler_params=params(L2),
    )(got, offsets, assignments, big)
    got = lax.all_to_all(sent, everyone, 0, 0, tiled=True)
    image, resid = pl.pallas_call(
        columns_back,
        out_shape=(
            jax.ShapeDtypeStruct((8, 32, 512), BF16),
            jax.ShapeDtypeStruct((1, SUB, SUB), BF16),
        ),
        in_specs=[VMEM, SMEM, VMEM, VMEM],
        out_specs=(VMEM, VMEM),
        scratch_shapes=[pltpu.VMEM((128, 8, 128), F32), pltpu.VMEM((128, 8, 128), F32)],
        compiler_params=params(16),
    )(got, offsets, jnp.asarray(twiddle), jnp.asarray(back))
    image = lax.all_to_all(image, "vis", 0, 0, tiled=True)
    return resid, image.reshape(256, 512).astype(F32)


def solution(mesh):
    placed = (P("facet", "vis"), P(("facet", "vis"), None, None), P(), P())
    return jax.shard_map(
        on_device,
        mesh=mesh,
        in_specs=placed,
        out_specs=(P(("facet", "vis"), None, None), P("facet", "vis")),
        check_vma=False,
    )
```

```python
import jax
import jax.numpy as jnp
import ml_dtypes
import numpy as np
from jax import lax
from jax.experimental import pallas as pl
from jax.experimental.pallas import tpu as pltpu
from jax.sharding import PartitionSpec as P

F32 = jnp.float32
BF16 = jnp.bfloat16
N = 4096
SUB = 256
HALF = 0.5**0.5
NT = (((1,), (1,)), ((), ()))


def turn(phase, period):
    angle = (2.0 * np.pi / period) * (phase % period)
    return np.cos(angle), np.sin(angle)


def bf(table):
    return table.astype(ml_dtypes.bfloat16)


def column_tables():
    order = np.arange(512)
    k1 = 16 * (order % 32) + order // 32
    c, s = turn(np.arange(512)[:, None] * k1[None, :], 512)
    ahead = bf(np.concatenate([c + s, c - s], axis=0) / 64.0)
    back = bf(np.concatenate([c.T, s.T], axis=1) / 16.0)
    c, s = turn(np.arange(8)[:, None] * np.arange(512)[None, :], N)
    return ahead, back, np.concatenate([c, s], axis=0).astype(np.float32)


def row_table():
    g = np.arange(N).reshape(16, 256)
    c, s = turn(g[:, :, None] * np.arange(SUB)[None, None, :], N)
    return bf(np.stack([c + s, c - s], axis=1).reshape(2 * N, SUB))


def own_index():
    return lax.axis_index("facet") * 8 + lax.axis_index("vis")


def lane_group(rows):
    return lax.broadcasted_iota(jnp.int32, (rows, 128), 1) >> 5


def swap_groups(parts, group):
    out = []
    for j in range(4):
        moved = [pltpu.roll(parts[i], (32 * (i - j)) % 128, 1) if i != j else parts[i] for i in range(4)]
        mixed = jnp.where(group < 2, jnp.where(group == 0, moved[0], moved[1]), jnp.where(group == 2, moved[2], moved[3]))
        out.append(mixed)
    return out


def selector(u):
    row = lax.broadcasted_iota(jnp.int32, (128, 128), 0)
    col = lax.broadcasted_iota(jnp.int32, (128, 128), 1)
    return jnp.where(((row - u) & 127) == col, 1.0, 0.0).astype(BF16)


def spin(re, im, c, s):
    return re * c - im * s, re * s + im * c


def cos_sin(phase):
    angle = (phase & (N - 1)).astype(F32) * np.float32(2.0 * np.pi / N)
    return jnp.cos(angle), jnp.sin(angle)


def tables(off_ref, asg_ref, ct_ref, st_ref, cg_ref, sg_ref, tc_ref, ts_ref, chosen_ref, bits_ref):
    me = own_index()
    v_row = jnp.broadcast_to(off_ref[1:2, :], (16, 128))
    step = lax.broadcasted_iota(jnp.int32, (16, 128), 0)
    lo_c, lo_s = cos_sin(v_row * step)
    hi_c, hi_s = cos_sin(v_row * step * 16)
    top_c, top_s = cos_sin(v_row * 256)
    pairs = [spin(lo_c, lo_s, hi_c[i : i + 1], hi_s[i : i + 1]) for i in range(16)]
    c = jnp.concatenate([p[0] for p in pairs], axis=0)
    s = jnp.concatenate([p[1] for p in pairs], axis=0)
    cg_ref[...], sg_ref[...] = c, s
    ct_ref[...], st_ref[...] = jnp.transpose(c), jnp.transpose(s)
    tc_ref[...], ts_ref[...] = top_c, top_s

    u = off_ref[0:1, :]
    first = (me - u) & 127
    s0 = ((u + first - me) >> 7) & 31
    lane = lax.broadcasted_iota(jnp.int32, (128, 128), 0) & 31
    for t in range(2):
        hit = jnp.where(lane == ((s0 + t) & 31), 1.0, 0.0)
        chosen_ref[128 * t : 128 * t + 128] = jnp.transpose(hit)
    asg = asg_ref[...]
    bits = jnp.sum(lax.shift_left(jnp.ones_like(asg), asg).astype(F32), axis=0, keepdims=True)
    bits_ref[...] = jnp.transpose(jnp.broadcast_to(bits, (128, 128))).astype(jnp.int32)


def round_image(sky_hbm, out_ref, held, sems):
    moves = [pltpu.make_async_copy(sky_hbm.at[pl.ds(64 * i, 64)], held.at[pl.ds(64 * i, 64)], sems.at[i]) for i in range(4)]
    for move in moves:
        move.start()
    for i, move in enumerate(moves):
        move.wait()
        out_ref[2 * i : 2 * i + 2] = held[64 * i : 64 * i + 64].reshape(2, 32, 512).astype(BF16)


def columns_ahead(rx_ref, obs_hbm, off_ref, big_hbm, out_ref, obs_ref, tab_ref, seen, sems):
    moves = [pltpu.make_async_copy(obs_hbm, obs_ref, sems.at[0])]
    for i in range(2):
        half = big_hbm.at[pl.ds(2 * N + 1024 * i, 1024)]
        moves.append(pltpu.make_async_copy(half, tab_ref.at[:, pl.ds(256 * i, 256)], sems.at[1 + i]))
    for move in moves:
        move.start()
    k2 = lax.broadcasted_iota(jnp.int32, (8, 512), 0)
    twist_c, twist_s = cos_sin(k2 * lax.broadcasted_iota(jnp.int32, (8, 512), 1))
    x = [rx_ref[j].astype(F32) for j in range(8)]
    e = [x[i] + x[i + 4] for i in range(4)]
    o = [x[i] - x[i + 4] for i in range(4)]
    up, down = (o[1] + o[3]) * HALF, (o[1] - o[3]) * HALF
    e02, e13 = e[0] + e[2], e[1] + e[3]
    d1 = (o[0] + down, o[2] + up)
    d2 = (e[0] - e[2], e[1] - e[3])
    d3 = (o[0] - down, up - o[2])
    spec = [(e02 + e13, None), d1, d2, d3, (e02 - e13, None), (d3[0], -d3[1]), (d2[0], -d2[1]), (d1[0], -d1[1])]
    rows = []
    for k2 in range(8):
        c, s = twist_c[k2 : k2 + 1], twist_s[k2 : k2 + 1]
        re, im = spec[k2]
        if im is None:
            zr, zi = re * c, re * s
        else:
            zr, zi = re * c - im * s, re * s + im * c
        rows.append(jnp.concatenate([zr, zi], axis=1))
    left = jnp.concatenate(rows, axis=0).astype(BF16)
    for move in moves:
        move.wait()
    freq = jnp.dot(left, tab_ref[...], preferred_element_type=F32)

    u = off_ref[0:1, :]
    place = lax.broadcasted_iota(jnp.int32, (1, 128), 1)
    u = jnp.sum(jnp.where(place == own_index(), u, 0).astype(F32), axis=1, keepdims=True).astype(jnp.int32)
    pick = selector(u)
    rows = seen.reshape(1024, 128)
    for t in range(2):
        for ah in range(2):
            quarter = obs_ref[0, 128 * ah : 128 * ah + 128, 128 * t : 128 * t + 128]
            cols = lax.dot_general(pick, quarter, NT, preferred_element_type=F32)
            rows[pl.ds(2 * t + ah, 128, stride=8), :] = cols
    group = lane_group(64)
    for qg in range(4):
        part = freq[:, 128 * qg : 128 * qg + 128].reshape(8, 4, 8, 128)
        tiles = swap_groups([part[:, rg].reshape(64, 128) for rg in range(4)], group)
        for q4 in range(4):
            at = 8 * (4 * qg + q4)
            tile = tiles[q4].reshape(8, 8, 128).astype(BF16)
            out_ref[at : at + 8, 0] = tile[:, 0:4]
            out_ref[at : at + 8, 1] = tile[:, 4:8]
            out_ref[at : at + 8, 2] = seen[at : at + 8][:, 0:4].astype(BF16)


def rows_kernel(
    rx_ref, off_ref, asg_ref, big_hbm,
    out_ref, ybuf, held, obs, rr, ct, st, cg, sg, tc_ref, ts_ref, chosen_ref, bits_ref, keep, zbuf, tab_ref, sem,
):
    fetch = pltpu.make_async_copy(big_hbm.at[pl.ds(0, 2 * N)], tab_ref, sem)
    fetch.start()
    tables(off_ref, asg_ref, ct, st, cg, sg, tc_ref, ts_ref, chosen_ref, bits_ref)
    group = lax.broadcasted_iota(jnp.int32, (8, 8, 128), 2) >> 5
    got = rx_ref[...].astype(F32)
    held[:, 0:4] = got[:, 0]
    held[:, 4:8] = got[:, 1]
    obs[:, 0:4] = got[:, 2]
    chosen = chosen_ref[...].astype(BF16)
    turn_c, turn_s = tc_ref[:8][None], ts_ref[:8][None]
    turn_ct = jnp.transpose(jnp.broadcast_to(tc_ref[:1], (256, 128)))
    turn_st = jnp.transpose(jnp.broadcast_to(ts_ref[:1], (256, 128)))

    @pl.loop(0, 16, unroll=UNROLL)
    def _(f):
        tile = held[pl.ds(8 * f, 8)]
        spread = jnp.stack([jnp.where(group == rg, tile, 0.0) for rg in range(4)], axis=1)
        right = spread.reshape(256, 128).astype(BF16)
        cols = lax.dot_general(chosen, right, NT, preferred_element_type=F32)
        at = pl.multiple_of(f * 256, 256)
        c, s = ct[...], st[...]
        for t in range(2):
            half = cols[128 * t : 128 * t + 128]
            ybuf[128 * t : 128 * t + 128, pl.ds(2 * at, 256)] = (half * c).astype(BF16)
            ybuf[128 * t : 128 * t + 128, pl.ds(2 * at + 256, 256)] = (half * s).astype(BF16)
        ct[...], st[...] = spin(c, s, turn_ct, turn_st)
        named = (lax.shift_right_logical(bits_ref[...], f) & 1) == 1
        for t in range(2):
            kept = jnp.where(named, chosen_ref[128 * t : 128 * t + 128], 0.0)
            keep[pl.ds(at + 128 * t, 128)] = kept.astype(BF16)

    fetch.wait()
    pred = jnp.dot(ybuf[...], tab_ref[...], preferred_element_type=F32) * (1.0 / 64.0)
    seen, back = obs.reshape(1024, 128), rr.reshape(1024, 128)
    resid = []
    for t in range(2):
        halves = []
        for ah in range(2):
            guess = pred[128 * t : 128 * t + 128, 128 * ah : 128 * ah + 128]
            quarter = seen[pl.ds(2 * t + ah, 128, stride=8), :] - guess
            halves.append(jnp.transpose(quarter))
            back[pl.ds(2 * t + ah, 128, stride=8), :] = quarter
        resid.append(jnp.concatenate(halves, axis=0))
    resid = jnp.concatenate(resid, axis=1).astype(BF16)

    @pl.loop(0, 16, unroll=UNROLL1)
    def _(f):
        at = pl.multiple_of(f * 256, 256)
        both = jnp.dot(tab_ref[pl.ds(2 * at, 512), :], resid, preferred_element_type=F32)
        c, s = cg[...], sg[...]
        z = [c * both[:256, 128 * t : 128 * t + 128] + s * both[256:, 128 * t : 128 * t + 128] for t in range(2)]
        zbuf[pl.ds(at, 256)] = jnp.concatenate(z, axis=1).astype(BF16)
        nc, ns = spin(c.reshape(32, 8, 128), s.reshape(32, 8, 128), turn_c, turn_s)
        cg[...], sg[...] = nc.reshape(256, 128), ns.reshape(256, 128)

    @pl.loop(0, 16, unroll=UNROLL2)
    def _(f):
        at = pl.multiple_of(f * 256, 256)
        grid = jnp.dot(zbuf[pl.ds(at, 256)], keep[pl.ds(at, 256)], preferred_element_type=F32).reshape(8, 4, 8, 128)
        mixed = jnp.where(
            group < 2,
            jnp.where(group == 0, grid[:, 0], grid[:, 1]),
            jnp.where(group == 2, grid[:, 2], grid[:, 3]),
        )
        mixed = (mixed * (1.0 / 16.0)).astype(BF16)
        out_ref[pl.ds(8 * f, 8), 0] = mixed[:, 0:4]
        out_ref[pl.ds(8 * f, 8), 1] = mixed[:, 4:8]
        out_ref[pl.ds(8 * f, 8), 2] = rr[pl.ds(8 * f, 8)][:, 0:4].astype(BF16)


def columns_back(rx_ref, off_ref, tw_ref, tab_ref, img_ref, res_ref, held, sent):
    got = rx_ref[...].astype(F32)
    held[:, 0:4] = got[:, 0]
    held[:, 4:8] = got[:, 1]
    tiles = held[...].reshape(16, 64, 128)
    group = lane_group(64)
    wide = [[None] * 4 for _ in range(4)]
    for qg in range(4):
        mixed = swap_groups([tiles[4 * qg + q4] for q4 in range(4)], group)
        for rg in range(4):
            wide[rg][qg] = mixed[rg].reshape(8, 8, 128)
    left = jnp.stack([jnp.concatenate(wide[rg], axis=2) for rg in range(4)], axis=1)
    left = left.reshape(256, 512).astype(BF16)
    both = jnp.dot(left, tab_ref[...], preferred_element_type=F32).reshape(8, 32, 1024)
    re, im = [], []
    for k2 in range(8):
        c, s = tw_ref[k2 : k2 + 1, :], tw_ref[8 + k2 : 9 + k2, :]
        a, b = spin(both[k2, :, :512], both[k2, :, 512:], c + s, s - c)
        re.append(a)
        im.append(b)
    a1, a2, a3 = re[1] + re[7], re[2] + re[6], re[3] + re[5]
    b1, b2, b3 = im[1] - im[7], im[2] - im[6], im[3] - im[5]
    plus, minus = re[0] + re[4], re[0] - re[4]
    even = [plus + a2, minus - b2, plus - a2, minus + b2]
    odd = [a1 + a3, HALF * (a1 - b1 - a3 - b3), b3 - b1, HALF * (a3 - a1 - b1 - b3)]
    for j in range(4):
        img_ref[j] = (even[j] + odd[j]).astype(BF16)
        img_ref[j + 4] = (even[j] - odd[j]).astype(BF16)

    u = off_ref[0, own_index()]
    sent[:, 0:4] = got[:, 2]
    rows = sent.reshape(1024, 128)
    pick = selector(u)
    for t in range(2):
        for ah in range(2):
            quarter = jnp.transpose(rows[pl.ds(2 * t + ah, 128, stride=8), :]).astype(BF16)
            quarter = jnp.dot(quarter, pick, preferred_element_type=F32).astype(BF16)
            res_ref[0, 128 * ah : 128 * ah + 128, 128 * t : 128 * t + 128] = quarter


VMEM = pl.BlockSpec(memory_space=pltpu.VMEM)
SMEM = pl.BlockSpec(memory_space=pltpu.SMEM)
HBM = pl.BlockSpec(memory_space=pltpu.HBM)
UNROLL, UNROLL1, UNROLL2 = 8, 8, 16
L0, L1, L2 = 53, 53, 53


def params(mebibytes):
    return pltpu.CompilerParams(vmem_limit_bytes=mebibytes * 2**20)


def on_device(sky_image, observed, offsets, assignments):
    ahead, back, twiddle = column_tables()
    big = jnp.asarray(np.concatenate([row_table(), ahead[:, :256], ahead[:, 256:]], axis=0))
    everyone = ("facet", "vis")
    message = jax.ShapeDtypeStruct((128, 3, 4, 128), BF16)
    offsets, assignments = offsets.T, assignments.T

    strips = pl.pallas_call(
        round_image,
        out_shape=jax.ShapeDtypeStruct((8, 32, 512), BF16),
        in_specs=[HBM],
        out_specs=VMEM,
        scratch_shapes=[pltpu.VMEM((256, 512), F32), pltpu.SemaphoreType.DMA((4,))],
        compiler_params=params(L0),
    )(sky_image)
    strips = lax.all_to_all(strips, "vis", 0, 0, tiled=True)
    sent = pl.pallas_call(
        columns_ahead,
        out_shape=message,
        in_specs=[VMEM, HBM, VMEM, HBM],
        out_specs=VMEM,
        scratch_shapes=[
            pltpu.VMEM((1, SUB, SUB), BF16),
            pltpu.VMEM((1024, 512), BF16),
            pltpu.VMEM((128, 8, 128), F32),
            pltpu.SemaphoreType.DMA((3,)),
        ],
        compiler_params=params(L1),
    )(strips, observed, offsets, big)
    got = lax.all_to_all(sent, everyone, 0, 0, tiled=True)
    sent = pl.pallas_call(
        rows_kernel,
        out_shape=message,
        in_specs=[VMEM, VMEM, VMEM, HBM],
        out_specs=VMEM,
        scratch_shapes=[
            pltpu.VMEM((256, 2 * N), BF16),
            pltpu.VMEM((128, 8, 128), F32),
            pltpu.VMEM((128, 8, 128), F32),
            pltpu.VMEM((128, 8, 128), F32),
            pltpu.VMEM((128, 256), F32),
            pltpu.VMEM((128, 256), F32),
            pltpu.VMEM((256, 128), F32),
            pltpu.VMEM((256, 128), F32),
            pltpu.VMEM((16, 128), F32),
            pltpu.VMEM((16, 128), F32),
            pltpu.VMEM((256, 128), F32),
            pltpu.VMEM((128, 128), jnp.int32),
            pltpu.VMEM((N, 128), BF16),
            pltpu.VMEM((N, 256), BF16),
            pltpu.VMEM((2 * N, 256), BF16),
            pltpu.SemaphoreType.DMA,
        ],
        compiler_params=params(L2),
    )(got, offsets, assignments, big)
    got = lax.all_to_all(sent, everyone, 0, 0, tiled=True)
    image, resid = pl.pallas_call(
        columns_back,
        out_shape=(
            jax.ShapeDtypeStruct((8, 32, 512), BF16),
            jax.ShapeDtypeStruct((1, SUB, SUB), BF16),
        ),
        in_specs=[VMEM, SMEM, VMEM, VMEM],
        out_specs=(VMEM, VMEM),
        scratch_shapes=[pltpu.VMEM((128, 8, 128), F32), pltpu.VMEM((128, 8, 128), F32)],
        compiler_params=params(16),
    )(got, offsets, jnp.asarray(twiddle), jnp.asarray(back))
    image = lax.all_to_all(image, "vis", 0, 0, tiled=True)
    return resid, image.reshape(256, 512).astype(F32)


def solution(mesh):
    placed = (P("facet", "vis"), P(("facet", "vis"), None, None), P(), P())
    return jax.shard_map(
        on_device,
        mesh=mesh,
        in_specs=placed,
        out_specs=(P(("facet", "vis"), None, None), P("facet", "vis")),
        check_vma=False,
    )
```

```python
import jax
import jax.numpy as jnp
import ml_dtypes
import numpy as np
from jax import lax
from jax.experimental import pallas as pl
from jax.experimental.pallas import tpu as pltpu
from jax.sharding import PartitionSpec as P

F32 = jnp.float32
BF16 = jnp.bfloat16
N = 4096
SUB = 256
HALF = 0.5**0.5
NT = (((1,), (1,)), ((), ()))


def turn(phase, period):
    angle = (2.0 * np.pi / period) * (phase % period)
    return np.cos(angle), np.sin(angle)


def bf(table):
    return table.astype(ml_dtypes.bfloat16)


def column_tables():
    order = np.arange(512)
    k1 = 16 * (order % 32) + order // 32
    c, s = turn(np.arange(512)[:, None] * k1[None, :], 512)
    ahead = bf(np.concatenate([c + s, c - s], axis=0) / 64.0)
    back = bf(np.concatenate([c.T, s.T], axis=1) / 16.0)
    c, s = turn(np.arange(8)[:, None] * np.arange(512)[None, :], N)
    return ahead, back, np.concatenate([c, s], axis=0).astype(np.float32)


def row_table():
    g = np.arange(N).reshape(16, 256)
    c, s = turn(g[:, :, None] * np.arange(SUB)[None, None, :], N)
    return bf(np.stack([c + s, c - s], axis=1).reshape(2 * N, SUB))


def own_index():
    return lax.axis_index("facet") * 8 + lax.axis_index("vis")


def lane_group(rows):
    return lax.broadcasted_iota(jnp.int32, (rows, 128), 1) >> 5


def swap_groups(parts, group):
    out = []
    for j in range(4):
        moved = [pltpu.roll(parts[i], (32 * (i - j)) % 128, 1) if i != j else parts[i] for i in range(4)]
        mixed = jnp.where(group < 2, jnp.where(group == 0, moved[0], moved[1]), jnp.where(group == 2, moved[2], moved[3]))
        out.append(mixed)
    return out


def selector(u):
    row = lax.broadcasted_iota(jnp.int32, (128, 128), 0)
    col = lax.broadcasted_iota(jnp.int32, (128, 128), 1)
    return jnp.where(((row - u) & 127) == col, 1.0, 0.0).astype(BF16)


def spin(re, im, c, s):
    return re * c - im * s, re * s + im * c


def cos_sin(phase):
    angle = (phase & (N - 1)).astype(F32) * np.float32(2.0 * np.pi / N)
    return jnp.cos(angle), jnp.sin(angle)


def tables(off_ref, asg_ref, ct_ref, st_ref, cg_ref, sg_ref, tc_ref, ts_ref, chosen_ref, keep_ref):
    me = own_index()
    v_row = jnp.broadcast_to(off_ref[1:2, :], (16, 128))
    step = lax.broadcasted_iota(jnp.int32, (16, 128), 0)
    lo_c, lo_s = cos_sin(v_row * step)
    hi_c, hi_s = cos_sin(v_row * step * 16)
    top_c, top_s = cos_sin(v_row * 256)
    pairs = [spin(lo_c, lo_s, hi_c[i : i + 1], hi_s[i : i + 1]) for i in range(16)]
    c = jnp.concatenate([p[0] for p in pairs], axis=0)
    s = jnp.concatenate([p[1] for p in pairs], axis=0)
    cg_ref[...], sg_ref[...] = c, s
    ct_ref[...], st_ref[...] = jnp.transpose(c), jnp.transpose(s)
    tc_ref[...], ts_ref[...] = top_c, top_s

    u = off_ref[0:1, :]
    first = (me - u) & 127
    s0 = ((u + first - me) >> 7) & 31
    lane = lax.broadcasted_iota(jnp.int32, (128, 128), 0) & 31
    chosen = [jnp.transpose(jnp.where(lane == ((s0 + t) & 31), 1.0, 0.0)) for t in range(2)]
    chosen_ref[...] = jnp.concatenate(chosen, axis=0).astype(BF16)
    asg = asg_ref[...]
    bits = jnp.sum(lax.shift_left(jnp.ones_like(asg), asg).astype(F32), axis=0, keepdims=True)
    bits = jnp.transpose(jnp.broadcast_to(bits, (128, 128))).astype(jnp.int32)
    for f in range(16):
        named = (lax.shift_right_logical(bits, f) & 1) == 1
        for t in range(2):
            at = 256 * f + 128 * t
            keep_ref[at : at + 128] = jnp.where(named, chosen[t], 0.0).astype(BF16)


def round_image(sky_hbm, out_hbm, held, done, sems):
    moves = [pltpu.make_async_copy(sky_hbm.at[pl.ds(64 * i, 64)], held.at[pl.ds(64 * i, 64)], sems.at[i]) for i in range(4)]
    backs = [pltpu.make_async_copy(done.at[pl.ds(2 * i, 2)], out_hbm.at[pl.ds(2 * i, 2)], sems.at[4 + i]) for i in range(4)]
    for move in moves:
        move.start()
    for i in range(4):
        moves[i].wait()
        done[2 * i : 2 * i + 2] = held[64 * i : 64 * i + 64].reshape(2, 32, 512).astype(BF16)
        backs[i].start()
    for back in backs:
        back.wait()


def observed_columns(obs_ref, off_ref, big_hbm, out_ref, tab_ref, seen, sems):
    moves = []
    for i in range(2):
        half = big_hbm.at[pl.ds(2 * N + 1024 * i, 1024)]
        moves.append(pltpu.make_async_copy(half, tab_ref.at[:, pl.ds(256 * i, 256)], sems.at[i]))
    for move in moves:
        move.start()
    u = off_ref[0:1, :]
    place = lax.broadcasted_iota(jnp.int32, (1, 128), 1)
    u = jnp.sum(jnp.where(place == own_index(), u, 0).astype(F32), axis=1, keepdims=True).astype(jnp.int32)
    pick = selector(u)
    rows = seen.reshape(1024, 128)
    for t in range(2):
        for ah in range(2):
            quarter = obs_ref[0, 128 * ah : 128 * ah + 128, 128 * t : 128 * t + 128]
            cols = lax.dot_general(pick, quarter, NT, preferred_element_type=F32)
            rows[pl.ds(2 * t + ah, 128, stride=8), :] = cols
    out_ref[...] = seen[...][:, 0:4].astype(BF16)
    for move in moves:
        move.wait()


def columns_ahead(rx_ref, seen_ref, tab_ref, out_hbm, out_ref, sems):
    k2 = lax.broadcasted_iota(jnp.int32, (8, 512), 0)
    twist_c, twist_s = cos_sin(k2 * lax.broadcasted_iota(jnp.int32, (8, 512), 1))
    x = [rx_ref[j].astype(F32) for j in range(8)]
    e = [x[i] + x[i + 4] for i in range(4)]
    o = [x[i] - x[i + 4] for i in range(4)]
    up, down = (o[1] + o[3]) * HALF, (o[1] - o[3]) * HALF
    e02, e13 = e[0] + e[2], e[1] + e[3]
    d1 = (o[0] + down, o[2] + up)
    d2 = (e[0] - e[2], e[1] - e[3])
    d3 = (o[0] - down, up - o[2])
    spec = [(e02 + e13, None), d1, d2, d3, (e02 - e13, None), (d3[0], -d3[1]), (d2[0], -d2[1]), (d1[0], -d1[1])]
    rows = []
    for k2 in range(8):
        c, s = twist_c[k2 : k2 + 1], twist_s[k2 : k2 + 1]
        re, im = spec[k2]
        if im is None:
            zr, zi = re * c, re * s
        else:
            zr, zi = re * c - im * s, re * s + im * c
        rows.append(jnp.concatenate([zr, zi], axis=1))
    left = jnp.concatenate(rows, axis=0).astype(BF16)
    freq = jnp.dot(left, tab_ref[...], preferred_element_type=F32)

    out_ref[:, 2] = seen_ref[...]
    leave = []
    group = lane_group(64)
    for qg in range(4):
        part = freq[:, 128 * qg : 128 * qg + 128].reshape(8, 4, 8, 128)
        tiles = swap_groups([part[:, rg].reshape(64, 128) for rg in range(4)], group)
        for q4 in range(4):
            at = 8 * (4 * qg + q4)
            tile = tiles[q4].reshape(8, 8, 128).astype(BF16)
            out_ref[at : at + 8, 0] = tile[:, 0:4]
            out_ref[at : at + 8, 1] = tile[:, 4:8]
        span = pl.ds(32 * qg, 32)
        leave.append(pltpu.make_async_copy(out_ref.at[span], out_hbm.at[span], sems.at[qg]))
        leave[qg].start()
    for move in leave:
        move.wait()


def rows_kernel(
    rx_ref, ct_ref, st_ref, cg_ref, sg_ref, tc_ref, ts_ref, chosen_ref, keep, big_hbm,
    out_ref, ybuf, held, obs, rr, ct, st, cg, sg, zbuf, tab_ref, sem,
):
    fetch = pltpu.make_async_copy(big_hbm.at[pl.ds(0, 2 * N)], tab_ref, sem)
    fetch.start()
    ct[...], st[...], cg[...], sg[...] = ct_ref[...], st_ref[...], cg_ref[...], sg_ref[...]
    group = lax.broadcasted_iota(jnp.int32, (8, 8, 128), 2) >> 5
    got = rx_ref[...].astype(F32)
    held[:, 0:4] = got[:, 0]
    held[:, 4:8] = got[:, 1]
    obs[:, 0:4] = got[:, 2]
    chosen = chosen_ref[...]
    turn_c, turn_s = tc_ref[:8][None], ts_ref[:8][None]
    turn_ct = jnp.transpose(jnp.broadcast_to(tc_ref[:1], (256, 128)))
    turn_st = jnp.transpose(jnp.broadcast_to(ts_ref[:1], (256, 128)))

    @pl.loop(0, 16, unroll=UNROLL)
    def _(f):
        tile = held[pl.ds(8 * f, 8)]
        spread = jnp.stack([jnp.where(group == rg, tile, 0.0) for rg in range(4)], axis=1)
        right = spread.reshape(256, 128).astype(BF16)
        cols = lax.dot_general(chosen, right, NT, preferred_element_type=F32)
        at = pl.multiple_of(f * 256, 256)
        c, s = ct[...], st[...]
        for t in range(2):
            half = cols[128 * t : 128 * t + 128]
            ybuf[128 * t : 128 * t + 128, pl.ds(2 * at, 256)] = (half * c).astype(BF16)
            ybuf[128 * t : 128 * t + 128, pl.ds(2 * at + 256, 256)] = (half * s).astype(BF16)
        ct[...], st[...] = spin(c, s, turn_ct, turn_st)

    fetch.wait()
    pred = jnp.dot(ybuf[...], tab_ref[...], preferred_element_type=F32) * (1.0 / 64.0)
    seen, back = obs.reshape(1024, 128), rr.reshape(1024, 128)
    resid = []
    for t in range(2):
        halves = []
        for ah in range(2):
            guess = pred[128 * t : 128 * t + 128, 128 * ah : 128 * ah + 128]
            quarter = seen[pl.ds(2 * t + ah, 128, stride=8), :] - guess
            halves.append(jnp.transpose(quarter))
            back[pl.ds(2 * t + ah, 128, stride=8), :] = quarter
        resid.append(jnp.concatenate(halves, axis=0))
    resid = jnp.concatenate(resid, axis=1).astype(BF16)

    @pl.loop(0, 16, unroll=UNROLL1)
    def _(f):
        at = pl.multiple_of(f * 256, 256)
        both = jnp.dot(tab_ref[pl.ds(2 * at, 512), :], resid, preferred_element_type=F32)
        c, s = cg[...], sg[...]
        z = [c * both[:256, 128 * t : 128 * t + 128] + s * both[256:, 128 * t : 128 * t + 128] for t in range(2)]
        zbuf[pl.ds(at, 256)] = jnp.concatenate(z, axis=1).astype(BF16)
        nc, ns = spin(c.reshape(32, 8, 128), s.reshape(32, 8, 128), turn_c, turn_s)
        cg[...], sg[...] = nc.reshape(256, 128), ns.reshape(256, 128)

    @pl.loop(0, 16, unroll=UNROLL2)
    def _(f):
        at = pl.multiple_of(f * 256, 256)
        grid = jnp.dot(zbuf[pl.ds(at, 256)], keep[pl.ds(at, 256)], preferred_element_type=F32).reshape(8, 4, 8, 128)
        mixed = jnp.where(
            group < 2,
            jnp.where(group == 0, grid[:, 0], grid[:, 1]),
            jnp.where(group == 2, grid[:, 2], grid[:, 3]),
        )
        mixed = (mixed * (1.0 / 16.0)).astype(BF16)
        out_ref[pl.ds(8 * f, 8), 0] = mixed[:, 0:4]
        out_ref[pl.ds(8 * f, 8), 1] = mixed[:, 4:8]
        out_ref[pl.ds(8 * f, 8), 2] = rr[pl.ds(8 * f, 8)][:, 0:4].astype(BF16)


def columns_back(rx_ref, tw_ref, tab_ref, img_hbm, held, img_ref, sems):
    got = rx_ref[...].astype(F32)
    held[:, 0:4] = got[:, 0]
    held[:, 4:8] = got[:, 1]
    tiles = held[...].reshape(16, 64, 128)
    group = lane_group(64)
    wide = [[None] * 4 for _ in range(4)]
    for qg in range(4):
        mixed = swap_groups([tiles[4 * qg + q4] for q4 in range(4)], group)
        for rg in range(4):
            wide[rg][qg] = mixed[rg].reshape(8, 8, 128)
    left = jnp.stack([jnp.concatenate(wide[rg], axis=2) for rg in range(4)], axis=1)
    left = left.reshape(256, 512).astype(BF16)
    both = jnp.dot(left, tab_ref[...], preferred_element_type=F32).reshape(8, 32, 1024)
    re, im = [], []
    for k2 in range(8):
        c, s = tw_ref[k2 : k2 + 1, :], tw_ref[8 + k2 : 9 + k2, :]
        a, b = spin(both[k2, :, :512], both[k2, :, 512:], c + s, s - c)
        re.append(a)
        im.append(b)
    a1, a2, a3 = re[1] + re[7], re[2] + re[6], re[3] + re[5]
    b1, b2, b3 = im[1] - im[7], im[2] - im[6], im[3] - im[5]
    plus, minus = re[0] + re[4], re[0] - re[4]
    even = [plus + a2, minus - b2, plus - a2, minus + b2]
    odd = [a1 + a3, HALF * (a1 - b1 - a3 - b3), b3 - b1, HALF * (a3 - a1 - b1 - b3)]
    leave = []
    for j in range(4):
        img_ref[j] = (even[j] + odd[j]).astype(BF16)
        img_ref[j + 4] = (even[j] - odd[j]).astype(BF16)
        for i in (j, j + 4):
            leave.append(pltpu.make_async_copy(img_ref.at[i], img_hbm.at[i], sems.at[i]))
            leave[-1].start()
    for move in leave:
        move.wait()


def residual_block(rx_ref, off_ref, res_ref, sent):
    u = off_ref[0, own_index()]
    sent[:, 0:4] = rx_ref[...].astype(F32)[:, 2]
    rows = sent.reshape(1024, 128)
    pick = selector(u)
    for t in range(2):
        for ah in range(2):
            quarter = jnp.transpose(rows[pl.ds(2 * t + ah, 128, stride=8), :]).astype(BF16)
            quarter = jnp.dot(quarter, pick, preferred_element_type=F32).astype(BF16)
            res_ref[0, 128 * ah : 128 * ah + 128, 128 * t : 128 * t + 128] = quarter


VMEM = pl.BlockSpec(memory_space=pltpu.VMEM)
SMEM = pl.BlockSpec(memory_space=pltpu.SMEM)
HBM = pl.BlockSpec(memory_space=pltpu.HBM)
UNROLL, UNROLL1, UNROLL2 = 8, 8, 16
L0, L1, L2 = 56, 50, 51


def params(mebibytes):
    return pltpu.CompilerParams(vmem_limit_bytes=mebibytes * 2**20)


def on_device(sky_image, observed, offsets, assignments):
    ahead, back, twiddle = column_tables()
    big = jnp.asarray(np.concatenate([row_table(), ahead[:, :256], ahead[:, 256:]], axis=0))
    everyone = ("facet", "vis")
    message = jax.ShapeDtypeStruct((128, 3, 4, 128), BF16)
    plan_shapes = [(128, 256), (128, 256), (256, 128), (256, 128), (16, 128), (16, 128)]
    offsets, assignments = offsets.T, assignments.T

    strips = pl.pallas_call(
        round_image,
        out_shape=jax.ShapeDtypeStruct((8, 32, 512), BF16),
        in_specs=[HBM],
        out_specs=HBM,
        scratch_shapes=[pltpu.VMEM((256, 512), F32), pltpu.VMEM((8, 32, 512), BF16), pltpu.SemaphoreType.DMA((8,))],
        compiler_params=params(L0),
    )(sky_image)
    strips = lax.all_to_all(strips, "vis", 0, 0, tiled=True)
    seen, ahead_table = pl.pallas_call(
        observed_columns,
        out_shape=(jax.ShapeDtypeStruct((128, 4, 128), BF16), jax.ShapeDtypeStruct((1024, 512), BF16)),
        in_specs=[VMEM, VMEM, HBM],
        out_specs=(VMEM, VMEM),
        scratch_shapes=[pltpu.VMEM((128, 8, 128), F32), pltpu.SemaphoreType.DMA((2,))],
        compiler_params=params(L1),
        cost_estimate=pl.CostEstimate(flops=10**9, bytes_accessed=4 * 10**6, transcendentals=0),
    )(observed, offsets, big)
    sent = pl.pallas_call(
        columns_ahead,
        out_shape=message,
        in_specs=[VMEM, VMEM, VMEM],
        out_specs=HBM,
        scratch_shapes=[pltpu.VMEM((128, 3, 4, 128), BF16), pltpu.SemaphoreType.DMA((4,))],
        compiler_params=params(32),
    )(strips, seen, ahead_table)
    got = lax.all_to_all(sent, everyone, 0, 0, tiled=True)
    plan = pl.pallas_call(
        tables,
        out_shape=(
            *[jax.ShapeDtypeStruct(shape, F32) for shape in plan_shapes],
            jax.ShapeDtypeStruct((256, 128), BF16),
            jax.ShapeDtypeStruct((N, 128), BF16),
        ),
        in_specs=[VMEM, VMEM],
        out_specs=(VMEM,) * 8,
        compiler_params=params(32),
        cost_estimate=pl.CostEstimate(flops=10**9, bytes_accessed=4 * 10**6, transcendentals=10**4),
    )(offsets, assignments)
    sent = pl.pallas_call(
        rows_kernel,
        out_shape=message,
        in_specs=[VMEM] * 9 + [HBM],
        out_specs=VMEM,
        scratch_shapes=[
            pltpu.VMEM((256, 2 * N), BF16),
            pltpu.VMEM((128, 8, 128), F32),
            pltpu.VMEM((128, 8, 128), F32),
            pltpu.VMEM((128, 8, 128), F32),
            pltpu.VMEM((128, 256), F32),
            pltpu.VMEM((128, 256), F32),
            pltpu.VMEM((256, 128), F32),
            pltpu.VMEM((256, 128), F32),
            pltpu.VMEM((N, 256), BF16),
            pltpu.VMEM((2 * N, 256), BF16),
            pltpu.SemaphoreType.DMA,
        ],
        compiler_params=params(L2),
    )(got, *plan, big)
    got = lax.all_to_all(sent, everyone, 0, 0, tiled=True)
    image = pl.pallas_call(
        columns_back,
        out_shape=jax.ShapeDtypeStruct((8, 32, 512), BF16),
        in_specs=[VMEM, VMEM, VMEM],
        out_specs=HBM,
        scratch_shapes=[
            pltpu.VMEM((128, 8, 128), F32),
            pltpu.VMEM((8, 32, 512), BF16),
            pltpu.SemaphoreType.DMA((8,)),
        ],
        compiler_params=params(16),
    )(got, jnp.asarray(twiddle), jnp.asarray(back))
    image = lax.all_to_all(image, "vis", 0, 0, tiled=True)
    resid = pl.pallas_call(
        residual_block,
        out_shape=jax.ShapeDtypeStruct((1, SUB, SUB), BF16),
        in_specs=[VMEM, SMEM],
        out_specs=VMEM,
        scratch_shapes=[pltpu.VMEM((128, 8, 128), F32)],
        compiler_params=params(16),
        cost_estimate=pl.CostEstimate(flops=10**9, bytes_accessed=4 * 10**6, transcendentals=0),
    )(got, offsets)
    return resid, image.reshape(256, 512).astype(F32)


def solution(mesh):
    placed = (P("facet", "vis"), P(("facet", "vis"), None, None), P(), P())
    return jax.shard_map(
        on_device,
        mesh=mesh,
        in_specs=placed,
        out_specs=(P(("facet", "vis"), None, None), P("facet", "vis")),
        check_vma=False,
    )
```

```python
import jax
import jax.numpy as jnp
import ml_dtypes
import numpy as np
from jax import lax
from jax.experimental import pallas as pl
from jax.experimental.pallas import tpu as pltpu
from jax.sharding import PartitionSpec as P

F32 = jnp.float32
BF16 = jnp.bfloat16
N = 4096
SUB = 256
HALF = 0.5**0.5
NT = (((1,), (1,)), ((), ()))


def turn(phase, period):
    angle = (2.0 * np.pi / period) * (phase % period)
    return np.cos(angle), np.sin(angle)


def bf(table):
    return table.astype(ml_dtypes.bfloat16)


def column_tables():
    order = np.arange(512)
    k1 = 16 * (order % 32) + order // 32
    c, s = turn(np.arange(512)[:, None] * k1[None, :], 512)
    ahead = bf(np.concatenate([c + s, c - s], axis=0) / 64.0)
    back = bf(np.concatenate([c.T, s.T], axis=1) / 16.0)
    c, s = turn(np.arange(8)[:, None] * np.arange(512)[None, :], N)
    return ahead, back, np.concatenate([c, s], axis=0).astype(np.float32)


def row_table():
    g = np.arange(N).reshape(16, 256)
    c, s = turn(g[:, :, None] * np.arange(SUB)[None, None, :], N)
    return bf(np.stack([c + s, c - s], axis=1).reshape(2 * N, SUB))


def own_index():
    return lax.axis_index("facet") * 8 + lax.axis_index("vis")


def lane_group(rows):
    return lax.broadcasted_iota(jnp.int32, (rows, 128), 1) >> 5


def swap_groups(parts, group):
    out = []
    for j in range(4):
        moved = [pltpu.roll(parts[i], (32 * (i - j)) % 128, 1) if i != j else parts[i] for i in range(4)]
        mixed = jnp.where(group < 2, jnp.where(group == 0, moved[0], moved[1]), jnp.where(group == 2, moved[2], moved[3]))
        out.append(mixed)
    return out


def own_column(off_ref):
    place = lax.broadcasted_iota(jnp.int32, (1, 128), 1)
    own = jnp.where(place == own_index(), off_ref[0:1, :], 0).astype(F32)
    return jnp.sum(own, axis=1, keepdims=True).astype(jnp.int32)


def selector(u):
    row = lax.broadcasted_iota(jnp.int32, (128, 128), 0)
    col = lax.broadcasted_iota(jnp.int32, (128, 128), 1)
    return jnp.where(((row - u) & 127) == col, 1.0, 0.0).astype(BF16)


def spin(re, im, c, s):
    return re * c - im * s, re * s + im * c


def cos_sin(phase):
    angle = (phase & (N - 1)).astype(F32) * np.float32(2.0 * np.pi / N)
    return jnp.cos(angle), jnp.sin(angle)


def tables(off_ref, asg_ref, ct_ref, st_ref, cg_ref, sg_ref, tc_ref, ts_ref, chosen_ref, bits_ref):
    me = own_index()
    v_row = jnp.broadcast_to(off_ref[1:2, :], (16, 128))
    step = lax.broadcasted_iota(jnp.int32, (16, 128), 0)
    lo_c, lo_s = cos_sin(v_row * step)
    hi_c, hi_s = cos_sin(v_row * step * 16)
    top_c, top_s = cos_sin(v_row * 256)
    pairs = [spin(lo_c, lo_s, hi_c[i : i + 1], hi_s[i : i + 1]) for i in range(16)]
    c = jnp.concatenate([p[0] for p in pairs], axis=0)
    s = jnp.concatenate([p[1] for p in pairs], axis=0)
    cg_ref[...], sg_ref[...] = c, s
    ct_ref[...], st_ref[...] = jnp.transpose(c), jnp.transpose(s)
    tc_ref[...], ts_ref[...] = top_c, top_s

    u = off_ref[0:1, :]
    first = (me - u) & 127
    s0 = ((u + first - me) >> 7) & 31
    lane = lax.broadcasted_iota(jnp.int32, (128, 128), 0) & 31
    for t in range(2):
        hit = jnp.where(lane == ((s0 + t) & 31), 1.0, 0.0)
        chosen_ref[128 * t : 128 * t + 128] = jnp.transpose(hit)
    asg = asg_ref[...]
    bits = jnp.sum(lax.shift_left(jnp.ones_like(asg), asg).astype(F32), axis=0, keepdims=True)
    bits_ref[...] = jnp.transpose(jnp.broadcast_to(bits, (128, 128))).astype(jnp.int32)


def round_image(sky_hbm, out_hbm, held, done, sems):
    moves = [pltpu.make_async_copy(sky_hbm.at[pl.ds(64 * i, 64)], held.at[pl.ds(64 * i, 64)], sems.at[i]) for i in range(4)]
    backs = [pltpu.make_async_copy(done.at[pl.ds(2 * i, 2)], out_hbm.at[pl.ds(2 * i, 2)], sems.at[4 + i]) for i in range(4)]
    for move in moves:
        move.start()
    for i in range(4):
        moves[i].wait()
        done[2 * i : 2 * i + 2] = held[64 * i : 64 * i + 64].reshape(2, 32, 512).astype(BF16)
        backs[i].start()
    for back in backs:
        back.wait()


def observed_columns(
    obs_ref, off_ref, asg_ref, big_hbm,
    out_ref, tab_ref, ct_ref, st_ref, cg_ref, sg_ref, tc_ref, ts_ref, chosen_ref, bits_ref, seen, sems,
):
    moves = []
    for i in range(2):
        half = big_hbm.at[pl.ds(2 * N + 1024 * i, 1024)]
        moves.append(pltpu.make_async_copy(half, tab_ref.at[:, pl.ds(256 * i, 256)], sems.at[i]))
    for move in moves:
        move.start()
    tables(off_ref, asg_ref, ct_ref, st_ref, cg_ref, sg_ref, tc_ref, ts_ref, chosen_ref, bits_ref)
    u = own_column(off_ref)
    pick = selector(u)
    rows = seen.reshape(1024, 128)
    for t in range(2):
        for ah in range(2):
            quarter = obs_ref[0, 128 * ah : 128 * ah + 128, 128 * t : 128 * t + 128]
            cols = lax.dot_general(pick, quarter, NT, preferred_element_type=F32)
            rows[pl.ds(2 * t + ah, 128, stride=8), :] = cols
    out_ref[...] = seen[...][:, 0:4].astype(BF16)
    for move in moves:
        move.wait()


def columns_ahead(rx_ref, seen_ref, tab_ref, out_ref):
    k2 = lax.broadcasted_iota(jnp.int32, (8, 512), 0)
    twist_c, twist_s = cos_sin(k2 * lax.broadcasted_iota(jnp.int32, (8, 512), 1))
    x = [rx_ref[j].astype(F32) for j in range(8)]
    e = [x[i] + x[i + 4] for i in range(4)]
    o = [x[i] - x[i + 4] for i in range(4)]
    up, down = (o[1] + o[3]) * HALF, (o[1] - o[3]) * HALF
    e02, e13 = e[0] + e[2], e[1] + e[3]
    d1 = (o[0] + down, o[2] + up)
    d2 = (e[0] - e[2], e[1] - e[3])
    d3 = (o[0] - down, up - o[2])
    spec = [(e02 + e13, None), d1, d2, d3, (e02 - e13, None), (d3[0], -d3[1]), (d2[0], -d2[1]), (d1[0], -d1[1])]
    rows = []
    for k2 in range(8):
        c, s = twist_c[k2 : k2 + 1], twist_s[k2 : k2 + 1]
        re, im = spec[k2]
        if im is None:
            zr, zi = re * c, re * s
        else:
            zr, zi = re * c - im * s, re * s + im * c
        rows.append(jnp.concatenate([zr, zi], axis=1))
    left = jnp.concatenate(rows, axis=0).astype(BF16)
    freq = jnp.dot(left, tab_ref[...], preferred_element_type=F32)

    out_ref[:, 2] = seen_ref[...]
    group = lane_group(64)
    for qg in range(4):
        part = freq[:, 128 * qg : 128 * qg + 128].reshape(8, 4, 8, 128)
        tiles = swap_groups([part[:, rg].reshape(64, 128) for rg in range(4)], group)
        for q4 in range(4):
            at = 8 * (4 * qg + q4)
            tile = tiles[q4].reshape(8, 8, 128).astype(BF16)
            out_ref[at : at + 8, 0] = tile[:, 0:4]
            out_ref[at : at + 8, 1] = tile[:, 4:8]


def rows_kernel(
    rx_ref, ct_ref, st_ref, cg_ref, sg_ref, tc_ref, ts_ref, chosen_ref, bits_ref, big_hbm,
    out_ref, ybuf, held, obs, rr, ct, st, cg, sg, keep, zbuf, tab_ref, sem,
):
    fetch = pltpu.make_async_copy(big_hbm.at[pl.ds(0, 2 * N)], tab_ref, sem)
    fetch.start()
    ct[...], st[...], cg[...], sg[...] = ct_ref[...], st_ref[...], cg_ref[...], sg_ref[...]
    group = lax.broadcasted_iota(jnp.int32, (8, 8, 128), 2) >> 5
    got = rx_ref[...].astype(F32)
    held[:, 0:4] = got[:, 0]
    held[:, 4:8] = got[:, 1]
    obs[:, 0:4] = got[:, 2]
    chosen = chosen_ref[...].astype(BF16)
    turn_c, turn_s = tc_ref[:8][None], ts_ref[:8][None]
    turn_ct = jnp.transpose(jnp.broadcast_to(tc_ref[:1], (256, 128)))
    turn_st = jnp.transpose(jnp.broadcast_to(ts_ref[:1], (256, 128)))

    @pl.loop(0, 16, unroll=UNROLL)
    def _(f):
        tile = held[pl.ds(8 * f, 8)]
        spread = jnp.stack([jnp.where(group == rg, tile, 0.0) for rg in range(4)], axis=1)
        right = spread.reshape(256, 128).astype(BF16)
        cols = lax.dot_general(chosen, right, NT, preferred_element_type=F32)
        at = pl.multiple_of(f * 256, 256)
        c, s = ct[...], st[...]
        for t in range(2):
            half = cols[128 * t : 128 * t + 128]
            ybuf[128 * t : 128 * t + 128, pl.ds(2 * at, 256)] = (half * c).astype(BF16)
            ybuf[128 * t : 128 * t + 128, pl.ds(2 * at + 256, 256)] = (half * s).astype(BF16)
        ct[...], st[...] = spin(c, s, turn_ct, turn_st)
        named = (lax.shift_right_logical(bits_ref[...], f) & 1) == 1
        for t in range(2):
            kept = jnp.where(named, chosen_ref[128 * t : 128 * t + 128], 0.0)
            keep[pl.ds(at + 128 * t, 128)] = kept.astype(BF16)

    fetch.wait()
    pred = jnp.dot(ybuf[...], tab_ref[...], preferred_element_type=F32) * (1.0 / 64.0)
    seen, back = obs.reshape(1024, 128), rr.reshape(1024, 128)
    resid = []
    for t in range(2):
        halves = []
        for ah in range(2):
            guess = pred[128 * t : 128 * t + 128, 128 * ah : 128 * ah + 128]
            quarter = seen[pl.ds(2 * t + ah, 128, stride=8), :] - guess
            halves.append(jnp.transpose(quarter))
            back[pl.ds(2 * t + ah, 128, stride=8), :] = quarter
        resid.append(jnp.concatenate(halves, axis=0))
    resid = jnp.concatenate(resid, axis=1).astype(BF16)

    @pl.loop(0, 16, unroll=UNROLL1)
    def _(f):
        at = pl.multiple_of(f * 256, 256)
        both = jnp.dot(tab_ref[pl.ds(2 * at, 512), :], resid, preferred_element_type=F32)
        c, s = cg[...], sg[...]
        z = [c * both[:256, 128 * t : 128 * t + 128] + s * both[256:, 128 * t : 128 * t + 128] for t in range(2)]
        zbuf[pl.ds(at, 256)] = jnp.concatenate(z, axis=1).astype(BF16)
        nc, ns = spin(c.reshape(32, 8, 128), s.reshape(32, 8, 128), turn_c, turn_s)
        cg[...], sg[...] = nc.reshape(256, 128), ns.reshape(256, 128)

    @pl.loop(0, 16, unroll=UNROLL2)
    def _(f):
        at = pl.multiple_of(f * 256, 256)
        grid = jnp.dot(zbuf[pl.ds(at, 256)], keep[pl.ds(at, 256)], preferred_element_type=F32).reshape(8, 4, 8, 128)
        mixed = jnp.where(
            group < 2,
            jnp.where(group == 0, grid[:, 0], grid[:, 1]),
            jnp.where(group == 2, grid[:, 2], grid[:, 3]),
        )
        mixed = (mixed * (1.0 / 16.0)).astype(BF16)
        out_ref[pl.ds(8 * f, 8), 0] = mixed[:, 0:4]
        out_ref[pl.ds(8 * f, 8), 1] = mixed[:, 4:8]
        out_ref[pl.ds(8 * f, 8), 2] = rr[pl.ds(8 * f, 8)][:, 0:4].astype(BF16)


def columns_back(rx_ref, off_ref, tw_ref, tab_ref, img_ref, res_hbm, held, sent, res_ref, sem):
    got = rx_ref[...].astype(F32)
    held[:, 0:4] = got[:, 0]
    held[:, 4:8] = got[:, 1]
    u = own_column(off_ref)
    sent[:, 0:4] = got[:, 2]
    rows = sent.reshape(1024, 128)
    pick = selector(u)
    for t in range(2):
        for ah in range(2):
            quarter = jnp.transpose(rows[pl.ds(2 * t + ah, 128, stride=8), :]).astype(BF16)
            quarter = jnp.dot(quarter, pick, preferred_element_type=F32).astype(BF16)
            res_ref[0, 128 * ah : 128 * ah + 128, 128 * t : 128 * t + 128] = quarter
    leave = pltpu.make_async_copy(res_ref, res_hbm, sem)
    leave.start()
    tiles = held[...].reshape(16, 64, 128)
    group = lane_group(64)
    wide = [[None] * 4 for _ in range(4)]
    for qg in range(4):
        mixed = swap_groups([tiles[4 * qg + q4] for q4 in range(4)], group)
        for rg in range(4):
            wide[rg][qg] = mixed[rg].reshape(8, 8, 128)
    left = jnp.stack([jnp.concatenate(wide[rg], axis=2) for rg in range(4)], axis=1)
    left = left.reshape(256, 512).astype(BF16)
    both = jnp.dot(left, tab_ref[...], preferred_element_type=F32).reshape(8, 32, 1024)
    re, im = [], []
    for k2 in range(8):
        c, s = tw_ref[k2 : k2 + 1, :], tw_ref[8 + k2 : 9 + k2, :]
        a, b = spin(both[k2, :, :512], both[k2, :, 512:], c + s, s - c)
        re.append(a)
        im.append(b)
    a1, a2, a3 = re[1] + re[7], re[2] + re[6], re[3] + re[5]
    b1, b2, b3 = im[1] - im[7], im[2] - im[6], im[3] - im[5]
    plus, minus = re[0] + re[4], re[0] - re[4]
    even = [plus + a2, minus - b2, plus - a2, minus + b2]
    odd = [a1 + a3, HALF * (a1 - b1 - a3 - b3), b3 - b1, HALF * (a3 - a1 - b1 - b3)]
    for j in range(4):
        img_ref[j] = (even[j] + odd[j]).astype(BF16)
        img_ref[j + 4] = (even[j] - odd[j]).astype(BF16)
    leave.wait()


VMEM = pl.BlockSpec(memory_space=pltpu.VMEM)
HBM = pl.BlockSpec(memory_space=pltpu.HBM)
UNROLL, UNROLL1, UNROLL2 = 8, 8, 16
L0, L1, L2 = 56, 50, 52


def params(mebibytes):
    return pltpu.CompilerParams(vmem_limit_bytes=mebibytes * 2**20)


def on_device(sky_image, observed, offsets, assignments):
    ahead, back, twiddle = column_tables()
    big = jnp.asarray(np.concatenate([row_table(), ahead[:, :256], ahead[:, 256:]], axis=0))
    everyone = ("facet", "vis")
    message = jax.ShapeDtypeStruct((128, 3, 4, 128), BF16)
    offsets, assignments = offsets.T, assignments.T

    strips = pl.pallas_call(
        round_image,
        out_shape=jax.ShapeDtypeStruct((8, 32, 512), BF16),
        in_specs=[HBM],
        out_specs=HBM,
        scratch_shapes=[pltpu.VMEM((256, 512), F32), pltpu.VMEM((8, 32, 512), BF16), pltpu.SemaphoreType.DMA((8,))],
        compiler_params=params(L0),
    )(sky_image)
    strips = lax.all_to_all(strips, "vis", 0, 0, tiled=True)
    plan_shapes = [(128, 256), (128, 256), (256, 128), (256, 128), (16, 128), (16, 128), (256, 128)]
    seen, ahead_table, *plan = pl.pallas_call(
        observed_columns,
        out_shape=(
            jax.ShapeDtypeStruct((128, 4, 128), BF16),
            jax.ShapeDtypeStruct((1024, 512), BF16),
            *[jax.ShapeDtypeStruct(shape, F32) for shape in plan_shapes],
            jax.ShapeDtypeStruct((128, 128), jnp.int32),
        ),
        in_specs=[VMEM, VMEM, VMEM, HBM],
        out_specs=(VMEM,) * 10,
        scratch_shapes=[pltpu.VMEM((128, 8, 128), F32), pltpu.SemaphoreType.DMA((2,))],
        compiler_params=params(L1),
        cost_estimate=pl.CostEstimate(flops=10**9, bytes_accessed=4 * 10**6, transcendentals=0),
    )(observed, offsets, assignments, big)
    sent = pl.pallas_call(
        columns_ahead,
        out_shape=message,
        in_specs=[VMEM, VMEM, VMEM],
        out_specs=VMEM,
        compiler_params=params(32),
    )(strips, seen, ahead_table)
    got = lax.all_to_all(sent, everyone, 0, 0, tiled=True)
    sent = pl.pallas_call(
        rows_kernel,
        out_shape=message,
        in_specs=[VMEM] * 9 + [HBM],
        out_specs=VMEM,
        scratch_shapes=[
            pltpu.VMEM((256, 2 * N), BF16),
            pltpu.VMEM((128, 8, 128), F32),
            pltpu.VMEM((128, 8, 128), F32),
            pltpu.VMEM((128, 8, 128), F32),
            pltpu.VMEM((128, 256), F32),
            pltpu.VMEM((128, 256), F32),
            pltpu.VMEM((256, 128), F32),
            pltpu.VMEM((256, 128), F32),
            pltpu.VMEM((N, 128), BF16),
            pltpu.VMEM((N, 256), BF16),
            pltpu.VMEM((2 * N, 256), BF16),
            pltpu.SemaphoreType.DMA,
        ],
        compiler_params=params(L2),
    )(got, *plan, big)
    got = lax.all_to_all(sent, everyone, 0, 0, tiled=True)
    image, resid = pl.pallas_call(
        columns_back,
        out_shape=(
            jax.ShapeDtypeStruct((8, 32, 512), BF16),
            jax.ShapeDtypeStruct((1, SUB, SUB), BF16),
        ),
        in_specs=[VMEM, VMEM, VMEM, VMEM],
        out_specs=(VMEM, HBM),
        scratch_shapes=[
            pltpu.VMEM((128, 8, 128), F32),
            pltpu.VMEM((128, 8, 128), F32),
            pltpu.VMEM((1, SUB, SUB), BF16),
            pltpu.SemaphoreType.DMA,
        ],
        compiler_params=params(16),
    )(got, offsets, jnp.asarray(twiddle), jnp.asarray(back))
    image = lax.all_to_all(image, "vis", 0, 0, tiled=True)
    return resid, image.reshape(256, 512).astype(F32)


def solution(mesh):
    placed = (P("facet", "vis"), P(("facet", "vis"), None, None), P(), P())
    return jax.shard_map(
        on_device,
        mesh=mesh,
        in_specs=placed,
        out_specs=(P(("facet", "vis"), None, None), P("facet", "vis")),
        check_vma=False,
    )
```

```python
import jax
import jax.numpy as jnp
import ml_dtypes
import numpy as np
from jax import lax
from jax.experimental import pallas as pl
from jax.experimental.pallas import tpu as pltpu
from jax.sharding import PartitionSpec as P

F32 = jnp.float32
BF16 = jnp.bfloat16
N = 4096
SUB = 256
HALF = 0.5**0.5
NT = (((1,), (1,)), ((), ()))


def turn(phase, period):
    angle = (2.0 * np.pi / period) * (phase % period)
    return np.cos(angle), np.sin(angle)


def bf(table):
    return table.astype(ml_dtypes.bfloat16)


def column_tables():
    order = np.arange(512)
    k1 = 16 * (order % 32) + order // 32
    c, s = turn(np.arange(512)[:, None] * k1[None, :], 512)
    ahead = bf(np.concatenate([c + s, c - s], axis=0) / 64.0)
    back = bf(np.concatenate([c.T, s.T], axis=1) / 16.0)
    c, s = turn(np.arange(8)[:, None] * np.arange(512)[None, :], N)
    return ahead, back, np.concatenate([c, s], axis=0).astype(np.float32)


def row_table():
    g = np.arange(N).reshape(16, 256)
    c, s = turn(g[:, :, None] * np.arange(SUB)[None, None, :], N)
    return bf(np.stack([c + s, c - s], axis=1).reshape(2 * N, SUB))


def own_index():
    return lax.axis_index("facet") * 8 + lax.axis_index("vis")


def lane_group(rows):
    return lax.broadcasted_iota(jnp.int32, (rows, 128), 1) >> 5


def swap_groups(parts, group):
    out = []
    for j in range(4):
        moved = [pltpu.roll(parts[i], (32 * (i - j)) % 128, 1) if i != j else parts[i] for i in range(4)]
        mixed = jnp.where(group < 2, jnp.where(group == 0, moved[0], moved[1]), jnp.where(group == 2, moved[2], moved[3]))
        out.append(mixed)
    return out


def own_column(off_ref):
    place = lax.broadcasted_iota(jnp.int32, (1, 128), 1)
    own = jnp.where(place == own_index(), off_ref[0:1, :], 0).astype(F32)
    return jnp.sum(own, axis=1, keepdims=True).astype(jnp.int32)


def selector(u):
    row = lax.broadcasted_iota(jnp.int32, (128, 128), 0)
    col = lax.broadcasted_iota(jnp.int32, (128, 128), 1)
    return jnp.where(((row - u) & 127) == col, 1.0, 0.0).astype(BF16)


def spin(re, im, c, s):
    return re * c - im * s, re * s + im * c


def cos_sin(phase):
    angle = (phase & (N - 1)).astype(F32) * np.float32(2.0 * np.pi / N)
    return jnp.cos(angle), jnp.sin(angle)


def tables(off_ref, asg_ref, ct_ref, st_ref, cg_ref, sg_ref, tc_ref, ts_ref, chosen_ref, bits_ref):
    me = own_index()
    v_row = jnp.broadcast_to(off_ref[1:2, :], (16, 128))
    step = lax.broadcasted_iota(jnp.int32, (16, 128), 0)
    lo_c, lo_s = cos_sin(v_row * step)
    hi_c, hi_s = cos_sin(v_row * step * 16)
    top_c, top_s = cos_sin(v_row * 256)
    pairs = [spin(lo_c, lo_s, hi_c[i : i + 1], hi_s[i : i + 1]) for i in range(16)]
    c = jnp.concatenate([p[0] for p in pairs], axis=0)
    s = jnp.concatenate([p[1] for p in pairs], axis=0)
    cg_ref[...], sg_ref[...] = c, s
    ct_ref[...], st_ref[...] = jnp.transpose(c), jnp.transpose(s)
    tc_ref[...], ts_ref[...] = top_c, top_s

    u = off_ref[0:1, :]
    first = (me - u) & 127
    s0 = ((u + first - me) >> 7) & 31
    lane = lax.broadcasted_iota(jnp.int32, (128, 128), 0) & 31
    for t in range(2):
        hit = jnp.where(lane == ((s0 + t) & 31), 1.0, 0.0)
        chosen_ref[128 * t : 128 * t + 128] = jnp.transpose(hit)
    asg = asg_ref[...]
    bits = jnp.sum(lax.shift_left(jnp.ones_like(asg), asg).astype(F32), axis=0, keepdims=True)
    bits_ref[...] = jnp.transpose(jnp.broadcast_to(bits, (128, 128))).astype(jnp.int32)


def round_image(sky_hbm, out_hbm, held, done, sems):
    rows = [pl.ds(128 * i, 128) for i in range(2)]
    strips = [pl.ds(4 * i, 4) for i in range(2)]
    moves = [pltpu.make_async_copy(sky_hbm.at[rows[i]], held.at[rows[i]], sems.at[i]) for i in range(2)]
    backs = [pltpu.make_async_copy(done.at[strips[i]], out_hbm.at[strips[i]], sems.at[2 + i]) for i in range(2)]
    for move in moves:
        move.start()
    for i in range(2):
        moves[i].wait()
        done[4 * i : 4 * i + 4] = held[128 * i : 128 * i + 128].reshape(4, 32, 512).astype(BF16)
        backs[i].start()
    for back in backs:
        back.wait()


def widen_image(img_ref, out_hbm, done, sems):
    rows = [pl.ds(64 * i, 64) for i in range(4)]
    leave = [pltpu.make_async_copy(done.at[rows[i]], out_hbm.at[rows[i]], sems.at[i]) for i in range(4)]
    for i in range(4):
        done[64 * i : 64 * i + 64] = img_ref[2 * i : 2 * i + 2].astype(F32).reshape(64, 512)
        leave[i].start()
    for move in leave:
        move.wait()


def observed_columns(
    obs_ref, off_ref, asg_ref, big_hbm,
    out_ref, tab_ref, ct_ref, st_ref, cg_ref, sg_ref, tc_ref, ts_ref, chosen_ref, bits_ref, seen, sems,
):
    moves = []
    for i in range(2):
        half = big_hbm.at[pl.ds(2 * N + 1024 * i, 1024)]
        moves.append(pltpu.make_async_copy(half, tab_ref.at[:, pl.ds(256 * i, 256)], sems.at[i]))
    for move in moves:
        move.start()
    tables(off_ref, asg_ref, ct_ref, st_ref, cg_ref, sg_ref, tc_ref, ts_ref, chosen_ref, bits_ref)
    u = own_column(off_ref)
    pick = selector(u)
    rows = seen.reshape(1024, 128)
    for t in range(2):
        for ah in range(2):
            quarter = obs_ref[0, 128 * ah : 128 * ah + 128, 128 * t : 128 * t + 128]
            cols = lax.dot_general(pick, quarter, NT, preferred_element_type=F32)
            rows[pl.ds(2 * t + ah, 128, stride=8), :] = cols
    out_ref[...] = seen[...][:, 0:4].astype(BF16)
    for move in moves:
        move.wait()


def columns_ahead(rx_ref, seen_ref, tab_ref, out_ref):
    k2 = lax.broadcasted_iota(jnp.int32, (8, 512), 0)
    twist_c, twist_s = cos_sin(k2 * lax.broadcasted_iota(jnp.int32, (8, 512), 1))
    x = [rx_ref[j].astype(F32) for j in range(8)]
    e = [x[i] + x[i + 4] for i in range(4)]
    o = [x[i] - x[i + 4] for i in range(4)]
    up, down = (o[1] + o[3]) * HALF, (o[1] - o[3]) * HALF
    e02, e13 = e[0] + e[2], e[1] + e[3]
    d1 = (o[0] + down, o[2] + up)
    d2 = (e[0] - e[2], e[1] - e[3])
    d3 = (o[0] - down, up - o[2])
    spec = [(e02 + e13, None), d1, d2, d3, (e02 - e13, None), (d3[0], -d3[1]), (d2[0], -d2[1]), (d1[0], -d1[1])]
    rows = []
    for k2 in range(8):
        c, s = twist_c[k2 : k2 + 1], twist_s[k2 : k2 + 1]
        re, im = spec[k2]
        if im is None:
            zr, zi = re * c, re * s
        else:
            zr, zi = re * c - im * s, re * s + im * c
        rows.append(jnp.concatenate([zr, zi], axis=1))
    left = jnp.concatenate(rows, axis=0).astype(BF16)
    freq = jnp.dot(left, tab_ref[...], preferred_element_type=F32)

    out_ref[:, 2] = seen_ref[...]
    group = lane_group(64)
    for qg in range(4):
        part = freq[:, 128 * qg : 128 * qg + 128].reshape(8, 4, 8, 128)
        tiles = swap_groups([part[:, rg].reshape(64, 128) for rg in range(4)], group)
        for q4 in range(4):
            at = 8 * (4 * qg + q4)
            tile = tiles[q4].reshape(8, 8, 128).astype(BF16)
            out_ref[at : at + 8, 0] = tile[:, 0:4]
            out_ref[at : at + 8, 1] = tile[:, 4:8]


def rows_kernel(
    rx_ref, ct_ref, st_ref, cg_ref, sg_ref, tc_ref, ts_ref, chosen_ref, bits_ref, big_hbm,
    out_ref, ybuf, held, obs, rr, ct, st, cg, sg, keep, zbuf, tab_ref, sem,
):
    fetch = pltpu.make_async_copy(big_hbm.at[pl.ds(0, 2 * N)], tab_ref, sem)
    fetch.start()
    ct[...], st[...], cg[...], sg[...] = ct_ref[...], st_ref[...], cg_ref[...], sg_ref[...]
    group = lax.broadcasted_iota(jnp.int32, (8, 8, 128), 2) >> 5
    got = rx_ref[...].astype(F32)
    held[:, 0:4] = got[:, 0]
    held[:, 4:8] = got[:, 1]
    obs[:, 0:4] = got[:, 2]
    chosen = chosen_ref[...].astype(BF16)
    turn_c, turn_s = tc_ref[:8][None], ts_ref[:8][None]
    turn_ct = jnp.transpose(jnp.broadcast_to(tc_ref[:1], (256, 128)))
    turn_st = jnp.transpose(jnp.broadcast_to(ts_ref[:1], (256, 128)))

    @pl.loop(0, 16, unroll=UNROLL)
    def _(f):
        tile = held[pl.ds(8 * f, 8)]
        spread = jnp.stack([jnp.where(group == rg, tile, 0.0) for rg in range(4)], axis=1)
        right = spread.reshape(256, 128).astype(BF16)
        cols = lax.dot_general(chosen, right, NT, preferred_element_type=F32)
        at = pl.multiple_of(f * 256, 256)
        c, s = ct[...], st[...]
        for t in range(2):
            half = cols[128 * t : 128 * t + 128]
            ybuf[128 * t : 128 * t + 128, pl.ds(2 * at, 256)] = (half * c).astype(BF16)
            ybuf[128 * t : 128 * t + 128, pl.ds(2 * at + 256, 256)] = (half * s).astype(BF16)
        ct[...], st[...] = spin(c, s, turn_ct, turn_st)
        named = (lax.shift_right_logical(bits_ref[...], f) & 1) == 1
        for t in range(2):
            kept = jnp.where(named, chosen_ref[128 * t : 128 * t + 128], 0.0)
            keep[pl.ds(at + 128 * t, 128)] = kept.astype(BF16)

    fetch.wait()
    pred = jnp.dot(ybuf[...], tab_ref[...], preferred_element_type=F32) * (1.0 / 64.0)
    seen, back = obs.reshape(1024, 128), rr.reshape(1024, 128)
    resid = []
    for t in range(2):
        halves = []
        for ah in range(2):
            guess = pred[128 * t : 128 * t + 128, 128 * ah : 128 * ah + 128]
            quarter = seen[pl.ds(2 * t + ah, 128, stride=8), :] - guess
            halves.append(jnp.transpose(quarter))
            back[pl.ds(2 * t + ah, 128, stride=8), :] = quarter
        resid.append(jnp.concatenate(halves, axis=0))
    resid = jnp.concatenate(resid, axis=1).astype(BF16)

    @pl.loop(0, 16, unroll=UNROLL1)
    def _(f):
        at = pl.multiple_of(f * 256, 256)
        both = jnp.dot(tab_ref[pl.ds(2 * at, 512), :], resid, preferred_element_type=F32)
        c, s = cg[...], sg[...]
        z = [c * both[:256, 128 * t : 128 * t + 128] + s * both[256:, 128 * t : 128 * t + 128] for t in range(2)]
        zbuf[pl.ds(at, 256)] = jnp.concatenate(z, axis=1).astype(BF16)
        nc, ns = spin(c.reshape(32, 8, 128), s.reshape(32, 8, 128), turn_c, turn_s)
        cg[...], sg[...] = nc.reshape(256, 128), ns.reshape(256, 128)

    @pl.loop(0, 16, unroll=UNROLL2)
    def _(f):
        at = pl.multiple_of(f * 256, 256)
        grid = jnp.dot(zbuf[pl.ds(at, 256)], keep[pl.ds(at, 256)], preferred_element_type=F32).reshape(8, 4, 8, 128)
        mixed = jnp.where(
            group < 2,
            jnp.where(group == 0, grid[:, 0], grid[:, 1]),
            jnp.where(group == 2, grid[:, 2], grid[:, 3]),
        )
        mixed = (mixed * (1.0 / 16.0)).astype(BF16)
        out_ref[pl.ds(8 * f, 8), 0] = mixed[:, 0:4]
        out_ref[pl.ds(8 * f, 8), 1] = mixed[:, 4:8]
        out_ref[pl.ds(8 * f, 8), 2] = rr[pl.ds(8 * f, 8)][:, 0:4].astype(BF16)


def columns_back(rx_ref, off_ref, tw_ref, tab_ref, img_ref, res_hbm, held, sent, res_ref, sem):
    got = rx_ref[...].astype(F32)
    held[:, 0:4] = got[:, 0]
    held[:, 4:8] = got[:, 1]
    u = own_column(off_ref)
    sent[:, 0:4] = got[:, 2]
    rows = sent.reshape(1024, 128)
    pick = selector(u)
    for t in range(2):
        for ah in range(2):
            quarter = jnp.transpose(rows[pl.ds(2 * t + ah, 128, stride=8), :]).astype(BF16)
            quarter = jnp.dot(quarter, pick, preferred_element_type=F32).astype(BF16)
            res_ref[0, 128 * ah : 128 * ah + 128, 128 * t : 128 * t + 128] = quarter
    leave = pltpu.make_async_copy(res_ref, res_hbm, sem)
    leave.start()
    tiles = held[...].reshape(16, 64, 128)
    group = lane_group(64)
    wide = [[None] * 4 for _ in range(4)]
    for qg in range(4):
        mixed = swap_groups([tiles[4 * qg + q4] for q4 in range(4)], group)
        for rg in range(4):
            wide[rg][qg] = mixed[rg].reshape(8, 8, 128)
    left = jnp.stack([jnp.concatenate(wide[rg], axis=2) for rg in range(4)], axis=1)
    left = left.reshape(256, 512).astype(BF16)
    both = jnp.dot(left, tab_ref[...], preferred_element_type=F32).reshape(8, 32, 1024)
    re, im = [], []
    for k2 in range(8):
        c, s = tw_ref[k2 : k2 + 1, :], tw_ref[8 + k2 : 9 + k2, :]
        a, b = spin(both[k2, :, :512], both[k2, :, 512:], c + s, s - c)
        re.append(a)
        im.append(b)
    a1, a2, a3 = re[1] + re[7], re[2] + re[6], re[3] + re[5]
    b1, b2, b3 = im[1] - im[7], im[2] - im[6], im[3] - im[5]
    plus, minus = re[0] + re[4], re[0] - re[4]
    even = [plus + a2, minus - b2, plus - a2, minus + b2]
    odd = [a1 + a3, HALF * (a1 - b1 - a3 - b3), b3 - b1, HALF * (a3 - a1 - b1 - b3)]
    for j in range(4):
        img_ref[j] = (even[j] + odd[j]).astype(BF16)
        img_ref[j + 4] = (even[j] - odd[j]).astype(BF16)
    leave.wait()


VMEM = pl.BlockSpec(memory_space=pltpu.VMEM)
HBM = pl.BlockSpec(memory_space=pltpu.HBM)
UNROLL, UNROLL1, UNROLL2 = 8, 8, 16
L0, L1, L2 = 56, 50, 52


def params(mebibytes):
    return pltpu.CompilerParams(vmem_limit_bytes=mebibytes * 2**20)


def on_device(sky_image, observed, offsets, assignments):
    ahead, back, twiddle = column_tables()
    big = jnp.asarray(np.concatenate([row_table(), ahead[:, :256], ahead[:, 256:]], axis=0))
    everyone = ("facet", "vis")
    message = jax.ShapeDtypeStruct((128, 3, 4, 128), BF16)
    offsets, assignments = offsets.T, assignments.T

    strips = pl.pallas_call(
        round_image,
        out_shape=jax.ShapeDtypeStruct((8, 32, 512), BF16),
        in_specs=[HBM],
        out_specs=HBM,
        scratch_shapes=[pltpu.VMEM((256, 512), F32), pltpu.VMEM((8, 32, 512), BF16), pltpu.SemaphoreType.DMA((4,))],
        compiler_params=params(L0),
    )(sky_image)
    strips = lax.all_to_all(strips, "vis", 0, 0, tiled=True)
    plan_shapes = [(128, 256), (128, 256), (256, 128), (256, 128), (16, 128), (16, 128), (256, 128)]
    seen, ahead_table, *plan = pl.pallas_call(
        observed_columns,
        out_shape=(
            jax.ShapeDtypeStruct((128, 4, 128), BF16),
            jax.ShapeDtypeStruct((1024, 512), BF16),
            *[jax.ShapeDtypeStruct(shape, F32) for shape in plan_shapes],
            jax.ShapeDtypeStruct((128, 128), jnp.int32),
        ),
        in_specs=[VMEM, VMEM, VMEM, HBM],
        out_specs=(VMEM,) * 10,
        scratch_shapes=[pltpu.VMEM((128, 8, 128), F32), pltpu.SemaphoreType.DMA((2,))],
        compiler_params=params(L1),
        cost_estimate=pl.CostEstimate(flops=10**9, bytes_accessed=4 * 10**6, transcendentals=0),
    )(observed, offsets, assignments, big)
    sent = pl.pallas_call(
        columns_ahead,
        out_shape=message,
        in_specs=[VMEM, VMEM, VMEM],
        out_specs=VMEM,
        compiler_params=params(32),
    )(strips, seen, ahead_table)
    got = lax.all_to_all(sent, everyone, 0, 0, tiled=True)
    sent = pl.pallas_call(
        rows_kernel,
        out_shape=message,
        in_specs=[VMEM] * 9 + [HBM],
        out_specs=VMEM,
        scratch_shapes=[
            pltpu.VMEM((256, 2 * N), BF16),
            pltpu.VMEM((128, 8, 128), F32),
            pltpu.VMEM((128, 8, 128), F32),
            pltpu.VMEM((128, 8, 128), F32),
            pltpu.VMEM((128, 256), F32),
            pltpu.VMEM((128, 256), F32),
            pltpu.VMEM((256, 128), F32),
            pltpu.VMEM((256, 128), F32),
            pltpu.VMEM((N, 128), BF16),
            pltpu.VMEM((N, 256), BF16),
            pltpu.VMEM((2 * N, 256), BF16),
            pltpu.SemaphoreType.DMA,
        ],
        compiler_params=params(L2),
    )(got, *plan, big)
    got = lax.all_to_all(sent, everyone, 0, 0, tiled=True)
    image, resid = pl.pallas_call(
        columns_back,
        out_shape=(
            jax.ShapeDtypeStruct((8, 32, 512), BF16),
            jax.ShapeDtypeStruct((1, SUB, SUB), BF16),
        ),
        in_specs=[VMEM, VMEM, VMEM, VMEM],
        out_specs=(VMEM, HBM),
        scratch_shapes=[
            pltpu.VMEM((128, 8, 128), F32),
            pltpu.VMEM((128, 8, 128), F32),
            pltpu.VMEM((1, SUB, SUB), BF16),
            pltpu.SemaphoreType.DMA,
        ],
        compiler_params=params(16),
    )(got, offsets, jnp.asarray(twiddle), jnp.asarray(back))
    image = lax.all_to_all(image, "vis", 0, 0, tiled=True)
    image = pl.pallas_call(
        widen_image,
        out_shape=jax.ShapeDtypeStruct((256, 512), F32),
        in_specs=[VMEM],
        out_specs=HBM,
        scratch_shapes=[pltpu.VMEM((256, 512), F32), pltpu.SemaphoreType.DMA((4,))],
        compiler_params=params(40),
    )(image)
    return resid, image


def solution(mesh):
    placed = (P("facet", "vis"), P(("facet", "vis"), None, None), P(), P())
    return jax.shard_map(
        on_device,
        mesh=mesh,
        in_specs=placed,
        out_specs=(P(("facet", "vis"), None, None), P("facet", "vis")),
        check_vma=False,
    )
```

```python
import jax
import jax.numpy as jnp
import ml_dtypes
import numpy as np
from jax import lax
from jax.experimental import pallas as pl
from jax.experimental.pallas import tpu as pltpu
from jax.sharding import PartitionSpec as P

F32 = jnp.float32
BF16 = jnp.bfloat16
N = 4096
SUB = 256
HALF = 0.5**0.5
NT = (((1,), (1,)), ((), ()))


def turn(phase, period):
    angle = (2.0 * np.pi / period) * (phase % period)
    return np.cos(angle), np.sin(angle)


def bf(table):
    return table.astype(ml_dtypes.bfloat16)


def column_tables():
    order = np.arange(512)
    k1 = 16 * (order % 32) + order // 32
    c, s = turn(np.arange(512)[:, None] * k1[None, :], 512)
    ahead = bf(np.concatenate([c + s, c - s], axis=0) / 64.0)
    back = bf(np.concatenate([c.T, s.T], axis=1) / 16.0)
    c, s = turn(np.arange(8)[:, None] * np.arange(512)[None, :], N)
    return ahead, back, np.concatenate([c, s], axis=0).astype(np.float32)


def row_table():
    g = np.arange(N).reshape(16, 256)
    c, s = turn(g[:, :, None] * np.arange(SUB)[None, None, :], N)
    return bf(np.stack([c + s, c - s], axis=1).reshape(2 * N, SUB))


def own_index():
    return lax.axis_index("facet") * 8 + lax.axis_index("vis")


def lane_group(rows):
    return lax.broadcasted_iota(jnp.int32, (rows, 128), 1) >> 5


def swap_groups(parts, group):
    out = []
    for j in range(4):
        moved = [pltpu.roll(parts[i], (32 * (i - j)) % 128, 1) if i != j else parts[i] for i in range(4)]
        mixed = jnp.where(group < 2, jnp.where(group == 0, moved[0], moved[1]), jnp.where(group == 2, moved[2], moved[3]))
        out.append(mixed)
    return out


def own_column(off_ref):
    place = lax.broadcasted_iota(jnp.int32, (1, 128), 1)
    own = jnp.where(place == own_index(), off_ref[0:1, :], 0).astype(F32)
    return jnp.sum(own, axis=1, keepdims=True).astype(jnp.int32)


def selector(u):
    row = lax.broadcasted_iota(jnp.int32, (128, 128), 0)
    col = lax.broadcasted_iota(jnp.int32, (128, 128), 1)
    return jnp.where(((row - u) & 127) == col, 1.0, 0.0).astype(BF16)


def spin(re, im, c, s):
    return re * c - im * s, re * s + im * c


def cos_sin(phase):
    angle = (phase & (N - 1)).astype(F32) * np.float32(2.0 * np.pi / N)
    return jnp.cos(angle), jnp.sin(angle)


def tables(off_ref, asg_ref, ct_ref, st_ref, cg_ref, sg_ref, tc_ref, ts_ref, chosen_ref, bits_ref):
    me = own_index()
    v_row = jnp.broadcast_to(off_ref[1:2, :], (16, 128))
    step = lax.broadcasted_iota(jnp.int32, (16, 128), 0)
    lo_c, lo_s = cos_sin(v_row * step)
    hi_c, hi_s = cos_sin(v_row * step * 16)
    top_c, top_s = cos_sin(v_row * 256)
    pairs = [spin(lo_c, lo_s, hi_c[i : i + 1], hi_s[i : i + 1]) for i in range(16)]
    c = jnp.concatenate([p[0] for p in pairs], axis=0)
    s = jnp.concatenate([p[1] for p in pairs], axis=0)
    cg_ref[...], sg_ref[...] = c, s
    ct_ref[...], st_ref[...] = jnp.transpose(c), jnp.transpose(s)
    tc_ref[...], ts_ref[...] = top_c, top_s

    u = off_ref[0:1, :]
    first = (me - u) & 127
    s0 = ((u + first - me) >> 7) & 31
    lane = lax.broadcasted_iota(jnp.int32, (128, 128), 0) & 31
    for t in range(2):
        hit = jnp.where(lane == ((s0 + t) & 31), 1.0, 0.0)
        chosen_ref[128 * t : 128 * t + 128] = jnp.transpose(hit)
    asg = asg_ref[...]
    bits = jnp.sum(lax.shift_left(jnp.ones_like(asg), asg).astype(F32), axis=0, keepdims=True)
    bits_ref[...] = jnp.transpose(jnp.broadcast_to(bits, (128, 128))).astype(jnp.int32)


def round_image(sky_hbm, out_hbm, held, done, sems):
    moves = [pltpu.make_async_copy(sky_hbm.at[pl.ds(64 * i, 64)], held.at[pl.ds(64 * i, 64)], sems.at[i]) for i in range(4)]
    backs = [pltpu.make_async_copy(done.at[pl.ds(2 * i, 2)], out_hbm.at[pl.ds(2 * i, 2)], sems.at[4 + i]) for i in range(4)]
    for move in moves:
        move.start()
    for i in range(4):
        moves[i].wait()
        done[2 * i : 2 * i + 2] = held[64 * i : 64 * i + 64].reshape(2, 32, 512).astype(BF16)
        backs[i].start()
    for back in backs:
        back.wait()


def observed_columns(
    obs_ref, off_ref, asg_ref, big_hbm,
    out_ref, tab_ref, ct_ref, st_ref, cg_ref, sg_ref, tc_ref, ts_ref, chosen_ref, bits_ref, seen, sems,
):
    moves = []
    for i in range(2):
        half = big_hbm.at[pl.ds(2 * N + 1024 * i, 1024)]
        moves.append(pltpu.make_async_copy(half, tab_ref.at[:, pl.ds(256 * i, 256)], sems.at[i]))
    for move in moves:
        move.start()
    tables(off_ref, asg_ref, ct_ref, st_ref, cg_ref, sg_ref, tc_ref, ts_ref, chosen_ref, bits_ref)
    u = own_column(off_ref)
    pick = selector(u)
    rows = seen.reshape(1024, 128)
    for t in range(2):
        for ah in range(2):
            quarter = obs_ref[0, 128 * ah : 128 * ah + 128, 128 * t : 128 * t + 128]
            cols = lax.dot_general(pick, quarter, NT, preferred_element_type=F32)
            rows[pl.ds(2 * t + ah, 128, stride=8), :] = cols
    out_ref[...] = seen[...][:, 0:4].astype(BF16)
    for move in moves:
        move.wait()


def columns_ahead(rx_ref, seen_ref, tab_ref, out_ref):
    k2 = lax.broadcasted_iota(jnp.int32, (8, 512), 0)
    twist_c, twist_s = cos_sin(k2 * lax.broadcasted_iota(jnp.int32, (8, 512), 1))
    x = [rx_ref[j].astype(F32) for j in range(8)]
    e = [x[i] + x[i + 4] for i in range(4)]
    o = [x[i] - x[i + 4] for i in range(4)]
    up, down = (o[1] + o[3]) * HALF, (o[1] - o[3]) * HALF
    e02, e13 = e[0] + e[2], e[1] + e[3]
    d1 = (o[0] + down, o[2] + up)
    d2 = (e[0] - e[2], e[1] - e[3])
    d3 = (o[0] - down, up - o[2])
    spec = [(e02 + e13, None), d1, d2, d3, (e02 - e13, None), (d3[0], -d3[1]), (d2[0], -d2[1]), (d1[0], -d1[1])]
    rows = []
    for k2 in range(8):
        c, s = twist_c[k2 : k2 + 1], twist_s[k2 : k2 + 1]
        re, im = spec[k2]
        if im is None:
            zr, zi = re * c, re * s
        else:
            zr, zi = re * c - im * s, re * s + im * c
        rows.append(jnp.concatenate([zr, zi], axis=1))
    left = jnp.concatenate(rows, axis=0).astype(BF16)
    freq = jnp.dot(left, tab_ref[...], preferred_element_type=F32)

    out_ref[:, 2] = seen_ref[...]
    group = lane_group(64)
    for qg in range(4):
        part = freq[:, 128 * qg : 128 * qg + 128].reshape(8, 4, 8, 128)
        tiles = swap_groups([part[:, rg].reshape(64, 128) for rg in range(4)], group)
        for q4 in range(4):
            at = 8 * (4 * qg + q4)
            tile = tiles[q4].reshape(8, 8, 128).astype(BF16)
            out_ref[at : at + 8, 0] = tile[:, 0:4]
            out_ref[at : at + 8, 1] = tile[:, 4:8]


def rows_kernel(
    rx_ref, ct_ref, st_ref, cg_ref, sg_ref, tc_ref, ts_ref, chosen_ref, bits_ref, big_hbm,
    out_ref, ybuf, held, obs, rr, ct, st, cg, sg, keep, zbuf, tab_ref, sem,
):
    fetch = pltpu.make_async_copy(big_hbm.at[pl.ds(0, 2 * N)], tab_ref, sem)
    fetch.start()
    ct[...], st[...], cg[...], sg[...] = ct_ref[...], st_ref[...], cg_ref[...], sg_ref[...]
    group = lax.broadcasted_iota(jnp.int32, (8, 8, 128), 2) >> 5
    got = rx_ref[...].astype(F32)
    held[:, 0:4] = got[:, 0]
    held[:, 4:8] = got[:, 1]
    obs[:, 0:4] = got[:, 2]
    chosen = chosen_ref[...].astype(BF16)
    turn_c, turn_s = tc_ref[:8][None], ts_ref[:8][None]
    turn_ct = jnp.transpose(jnp.broadcast_to(tc_ref[:1], (256, 128)))
    turn_st = jnp.transpose(jnp.broadcast_to(ts_ref[:1], (256, 128)))

    group2 = lax.broadcasted_iota(jnp.int32, (16, 8, 128), 2) >> 5

    @pl.loop(0, 8, unroll=UNROLL)
    def _(pair):
        tile = held[pl.ds(16 * pair, 16)]
        spread = jnp.stack([jnp.where(group2 == rg, tile, 0.0) for rg in range(4)], axis=1)
        right = spread.reshape(512, 128).astype(BF16)
        cols = lax.dot_general(chosen, right, NT, preferred_element_type=F32)
        c, s = ct[...], st[...]
        for i in range(2):
            at = pl.multiple_of(pair * 512 + 256 * i, 256)
            for t in range(2):
                half = cols[128 * t : 128 * t + 128, 256 * i : 256 * i + 256]
                ybuf[128 * t : 128 * t + 128, pl.ds(2 * at, 256)] = (half * c).astype(BF16)
                ybuf[128 * t : 128 * t + 128, pl.ds(2 * at + 256, 256)] = (half * s).astype(BF16)
            c, s = spin(c, s, turn_ct, turn_st)
            named = (lax.shift_right_logical(bits_ref[...], 2 * pair + i) & 1) == 1
            for t in range(2):
                kept = jnp.where(named, chosen_ref[128 * t : 128 * t + 128], 0.0)
                keep[pl.ds(at + 128 * t, 128)] = kept.astype(BF16)
        ct[...], st[...] = c, s

    fetch.wait()
    pred = jnp.dot(ybuf[...], tab_ref[...], preferred_element_type=F32) * (1.0 / 64.0)
    seen, back = obs.reshape(1024, 128), rr.reshape(1024, 128)
    resid = []
    for t in range(2):
        halves = []
        for ah in range(2):
            guess = pred[128 * t : 128 * t + 128, 128 * ah : 128 * ah + 128]
            quarter = seen[pl.ds(2 * t + ah, 128, stride=8), :] - guess
            halves.append(jnp.transpose(quarter))
            back[pl.ds(2 * t + ah, 128, stride=8), :] = quarter
        resid.append(jnp.concatenate(halves, axis=0))
    resid = jnp.concatenate(resid, axis=1).astype(BF16)

    @pl.loop(0, 16, unroll=UNROLL1)
    def _(f):
        at = pl.multiple_of(f * 256, 256)
        both = jnp.dot(tab_ref[pl.ds(2 * at, 512), :], resid, preferred_element_type=F32)
        c, s = cg[...], sg[...]
        z = [c * both[:256, 128 * t : 128 * t + 128] + s * both[256:, 128 * t : 128 * t + 128] for t in range(2)]
        zbuf[pl.ds(at, 256)] = jnp.concatenate(z, axis=1).astype(BF16)
        nc, ns = spin(c.reshape(32, 8, 128), s.reshape(32, 8, 128), turn_c, turn_s)
        cg[...], sg[...] = nc.reshape(256, 128), ns.reshape(256, 128)

    @pl.loop(0, 16, unroll=UNROLL2)
    def _(f):
        at = pl.multiple_of(f * 256, 256)
        grid = jnp.dot(zbuf[pl.ds(at, 256)], keep[pl.ds(at, 256)], preferred_element_type=F32).reshape(8, 4, 8, 128)
        mixed = jnp.where(
            group < 2,
            jnp.where(group == 0, grid[:, 0], grid[:, 1]),
            jnp.where(group == 2, grid[:, 2], grid[:, 3]),
        )
        mixed = (mixed * (1.0 / 16.0)).astype(BF16)
        out_ref[pl.ds(8 * f, 8), 0] = mixed[:, 0:4]
        out_ref[pl.ds(8 * f, 8), 1] = mixed[:, 4:8]
        out_ref[pl.ds(8 * f, 8), 2] = rr[pl.ds(8 * f, 8)][:, 0:4].astype(BF16)


def columns_back(rx_ref, off_ref, tw_ref, tab_ref, img_ref, res_hbm, held, sent, res_ref, sem):
    got = rx_ref[...].astype(F32)
    held[:, 0:4] = got[:, 0]
    held[:, 4:8] = got[:, 1]
    u = own_column(off_ref)
    sent[:, 0:4] = got[:, 2]
    rows = sent.reshape(1024, 128)
    pick = selector(u)
    for t in range(2):
        for ah in range(2):
            quarter = jnp.transpose(rows[pl.ds(2 * t + ah, 128, stride=8), :]).astype(BF16)
            quarter = jnp.dot(quarter, pick, preferred_element_type=F32).astype(BF16)
            res_ref[0, 128 * ah : 128 * ah + 128, 128 * t : 128 * t + 128] = quarter
    leave = pltpu.make_async_copy(res_ref, res_hbm, sem)
    leave.start()
    tiles = held[...].reshape(16, 64, 128)
    group = lane_group(64)
    wide = [[None] * 4 for _ in range(4)]
    for qg in range(4):
        mixed = swap_groups([tiles[4 * qg + q4] for q4 in range(4)], group)
        for rg in range(4):
            wide[rg][qg] = mixed[rg].reshape(8, 8, 128)
    left = jnp.stack([jnp.concatenate(wide[rg], axis=2) for rg in range(4)], axis=1)
    left = left.reshape(256, 512).astype(BF16)
    both = jnp.dot(left, tab_ref[...], preferred_element_type=F32).reshape(8, 32, 1024)
    re, im = [], []
    for k2 in range(8):
        c, s = tw_ref[k2 : k2 + 1, :], tw_ref[8 + k2 : 9 + k2, :]
        a, b = spin(both[k2, :, :512], both[k2, :, 512:], c + s, s - c)
        re.append(a)
        im.append(b)
    a1, a2, a3 = re[1] + re[7], re[2] + re[6], re[3] + re[5]
    b1, b2, b3 = im[1] - im[7], im[2] - im[6], im[3] - im[5]
    plus, minus = re[0] + re[4], re[0] - re[4]
    even = [plus + a2, minus - b2, plus - a2, minus + b2]
    odd = [a1 + a3, HALF * (a1 - b1 - a3 - b3), b3 - b1, HALF * (a3 - a1 - b1 - b3)]
    for j in range(4):
        img_ref[j] = (even[j] + odd[j]).astype(BF16)
        img_ref[j + 4] = (even[j] - odd[j]).astype(BF16)
    leave.wait()


VMEM = pl.BlockSpec(memory_space=pltpu.VMEM)
HBM = pl.BlockSpec(memory_space=pltpu.HBM)
UNROLL, UNROLL1, UNROLL2 = 4, 8, 16
L0, L1, L2 = 56, 50, 52


def params(mebibytes):
    return pltpu.CompilerParams(vmem_limit_bytes=mebibytes * 2**20)


def on_device(sky_image, observed, offsets, assignments):
    ahead, back, twiddle = column_tables()
    big = jnp.asarray(np.concatenate([row_table(), ahead[:, :256], ahead[:, 256:]], axis=0))
    everyone = ("facet", "vis")
    message = jax.ShapeDtypeStruct((128, 3, 4, 128), BF16)
    offsets, assignments = offsets.T, assignments.T

    strips = pl.pallas_call(
        round_image,
        out_shape=jax.ShapeDtypeStruct((8, 32, 512), BF16),
        in_specs=[HBM],
        out_specs=HBM,
        scratch_shapes=[pltpu.VMEM((256, 512), F32), pltpu.VMEM((8, 32, 512), BF16), pltpu.SemaphoreType.DMA((8,))],
        compiler_params=params(L0),
    )(sky_image)
    strips = lax.all_to_all(strips, "vis", 0, 0, tiled=True)
    plan_shapes = [(128, 256), (128, 256), (256, 128), (256, 128), (16, 128), (16, 128), (256, 128)]
    seen, ahead_table, *plan = pl.pallas_call(
        observed_columns,
        out_shape=(
            jax.ShapeDtypeStruct((128, 4, 128), BF16),
            jax.ShapeDtypeStruct((1024, 512), BF16),
            *[jax.ShapeDtypeStruct(shape, F32) for shape in plan_shapes],
            jax.ShapeDtypeStruct((128, 128), jnp.int32),
        ),
        in_specs=[VMEM, VMEM, VMEM, HBM],
        out_specs=(VMEM,) * 10,
        scratch_shapes=[pltpu.VMEM((128, 8, 128), F32), pltpu.SemaphoreType.DMA((2,))],
        compiler_params=params(L1),
        cost_estimate=pl.CostEstimate(flops=10**9, bytes_accessed=4 * 10**6, transcendentals=0),
    )(observed, offsets, assignments, big)
    sent = pl.pallas_call(
        columns_ahead,
        out_shape=message,
        in_specs=[VMEM, VMEM, VMEM],
        out_specs=VMEM,
        compiler_params=params(32),
    )(strips, seen, ahead_table)
    got = lax.all_to_all(sent, everyone, 0, 0, tiled=True)
    sent = pl.pallas_call(
        rows_kernel,
        out_shape=message,
        in_specs=[VMEM] * 9 + [HBM],
        out_specs=VMEM,
        scratch_shapes=[
            pltpu.VMEM((256, 2 * N), BF16),
            pltpu.VMEM((128, 8, 128), F32),
            pltpu.VMEM((128, 8, 128), F32),
            pltpu.VMEM((128, 8, 128), F32),
            pltpu.VMEM((128, 256), F32),
            pltpu.VMEM((128, 256), F32),
            pltpu.VMEM((256, 128), F32),
            pltpu.VMEM((256, 128), F32),
            pltpu.VMEM((N, 128), BF16),
            pltpu.VMEM((N, 256), BF16),
            pltpu.VMEM((2 * N, 256), BF16),
            pltpu.SemaphoreType.DMA,
        ],
        compiler_params=params(L2),
    )(got, *plan, big)
    got = lax.all_to_all(sent, everyone, 0, 0, tiled=True)
    image, resid = pl.pallas_call(
        columns_back,
        out_shape=(
            jax.ShapeDtypeStruct((8, 32, 512), BF16),
            jax.ShapeDtypeStruct((1, SUB, SUB), BF16),
        ),
        in_specs=[VMEM, VMEM, VMEM, VMEM],
        out_specs=(VMEM, HBM),
        scratch_shapes=[
            pltpu.VMEM((128, 8, 128), F32),
            pltpu.VMEM((128, 8, 128), F32),
            pltpu.VMEM((1, SUB, SUB), BF16),
            pltpu.SemaphoreType.DMA,
        ],
        compiler_params=params(16),
    )(got, offsets, jnp.asarray(twiddle), jnp.asarray(back))
    image = lax.all_to_all(image, "vis", 0, 0, tiled=True)
    return resid, image.reshape(256, 512).astype(F32)


def solution(mesh):
    placed = (P("facet", "vis"), P(("facet", "vis"), None, None), P(), P())
    return jax.shard_map(
        on_device,
        mesh=mesh,
        in_specs=placed,
        out_specs=(P(("facet", "vis"), None, None), P("facet", "vis")),
        check_vma=False,
    )
```

```python
import jax
import jax.numpy as jnp
import ml_dtypes
import numpy as np
from jax import lax
from jax.experimental import pallas as pl
from jax.experimental.pallas import tpu as pltpu
from jax.sharding import PartitionSpec as P

F32 = jnp.float32
BF16 = jnp.bfloat16
N = 4096
SUB = 256
HALF = 0.5**0.5
NT = (((1,), (1,)), ((), ()))


def turn(phase, period):
    angle = (2.0 * np.pi / period) * (phase % period)
    return np.cos(angle), np.sin(angle)


def bf(table):
    return table.astype(ml_dtypes.bfloat16)


def column_tables():
    order = np.arange(512)
    k1 = 16 * (order % 32) + order // 32
    c, s = turn(np.arange(512)[:, None] * k1[None, :], 512)
    ahead = bf(np.concatenate([c + s, c - s], axis=0) / 64.0)
    back = bf(np.concatenate([c.T, s.T], axis=1) / 16.0)
    c, s = turn(np.arange(8)[:, None] * np.arange(512)[None, :], N)
    return ahead, back, np.concatenate([c, s], axis=0).astype(np.float32)


def row_table():
    g = np.arange(N).reshape(16, 256)
    c, s = turn(g[:, :, None] * np.arange(SUB)[None, None, :], N)
    return bf(np.stack([c + s, c - s], axis=1).reshape(2 * N, SUB))


def own_index():
    return lax.axis_index("facet") * 8 + lax.axis_index("vis")


def lane_group(rows):
    return lax.broadcasted_iota(jnp.int32, (rows, 128), 1) >> 5


def swap_groups(parts, group):
    out = []
    for j in range(4):
        moved = [pltpu.roll(parts[i], (32 * (i - j)) % 128, 1) if i != j else parts[i] for i in range(4)]
        mixed = jnp.where(group < 2, jnp.where(group == 0, moved[0], moved[1]), jnp.where(group == 2, moved[2], moved[3]))
        out.append(mixed)
    return out


def own_column(off_ref):
    place = lax.broadcasted_iota(jnp.int32, (1, 128), 1)
    own = jnp.where(place == own_index(), off_ref[0:1, :], 0).astype(F32)
    return jnp.sum(own, axis=1, keepdims=True).astype(jnp.int32)


def selector(u):
    row = lax.broadcasted_iota(jnp.int32, (128, 128), 0)
    col = lax.broadcasted_iota(jnp.int32, (128, 128), 1)
    return jnp.where(((row - u) & 127) == col, 1.0, 0.0).astype(BF16)


def spin(re, im, c, s):
    return re * c - im * s, re * s + im * c


def cos_sin(phase):
    angle = (phase & (N - 1)).astype(F32) * np.float32(2.0 * np.pi / N)
    return jnp.cos(angle), jnp.sin(angle)


def tables(off_ref, asg_ref, ct_ref, st_ref, cg_ref, sg_ref, tc_ref, ts_ref, chosen_ref, bits_ref):
    me = own_index()
    v_row = jnp.broadcast_to(off_ref[1:2, :], (16, 128))
    step = lax.broadcasted_iota(jnp.int32, (16, 128), 0)
    lo_c, lo_s = cos_sin(v_row * step)
    hi_c, hi_s = cos_sin(v_row * step * 16)
    top_c, top_s = cos_sin(v_row * 256)
    pairs = [spin(lo_c, lo_s, hi_c[i : i + 1], hi_s[i : i + 1]) for i in range(16)]
    c = jnp.concatenate([p[0] for p in pairs], axis=0)
    s = jnp.concatenate([p[1] for p in pairs], axis=0)
    cg_ref[...], sg_ref[...] = c, s
    ct_ref[...], st_ref[...] = jnp.transpose(c), jnp.transpose(s)
    tc_ref[...], ts_ref[...] = top_c, top_s

    u = off_ref[0:1, :]
    first = (me - u) & 127
    s0 = ((u + first - me) >> 7) & 31
    lane = lax.broadcasted_iota(jnp.int32, (128, 128), 0) & 31
    for t in range(2):
        hit = jnp.where(lane == ((s0 + t) & 31), 1.0, 0.0)
        chosen_ref[128 * t : 128 * t + 128] = jnp.transpose(hit)
    asg = asg_ref[...]
    bits = jnp.sum(lax.shift_left(jnp.ones_like(asg), asg).astype(F32), axis=0, keepdims=True)
    bits_ref[...] = jnp.transpose(jnp.broadcast_to(bits, (128, 128))).astype(jnp.int32)


def round_image(sky_hbm, out_hbm, held, done, sems):
    moves = [pltpu.make_async_copy(sky_hbm.at[pl.ds(64 * i, 64)], held.at[pl.ds(64 * i, 64)], sems.at[i]) for i in range(4)]
    backs = [pltpu.make_async_copy(done.at[pl.ds(2 * i, 2)], out_hbm.at[pl.ds(2 * i, 2)], sems.at[4 + i]) for i in range(4)]
    for move in moves:
        move.start()
    for i in range(4):
        moves[i].wait()
        done[2 * i : 2 * i + 2] = held[64 * i : 64 * i + 64].reshape(2, 32, 512).astype(BF16)
        backs[i].start()
    for back in backs:
        back.wait()


def observed_columns(
    obs_ref, off_ref, asg_ref, big_hbm,
    out_ref, tab_ref, ct_ref, st_ref, cg_ref, sg_ref, tc_ref, ts_ref, chosen_ref, bits_ref, seen, sems,
):
    moves = []
    for i in range(2):
        half = big_hbm.at[pl.ds(2 * N + 1024 * i, 1024)]
        moves.append(pltpu.make_async_copy(half, tab_ref.at[:, pl.ds(256 * i, 256)], sems.at[i]))
    for move in moves:
        move.start()
    tables(off_ref, asg_ref, ct_ref, st_ref, cg_ref, sg_ref, tc_ref, ts_ref, chosen_ref, bits_ref)
    u = own_column(off_ref)
    pick = selector(u)
    rows = seen.reshape(1024, 128)
    for t in range(2):
        for ah in range(2):
            quarter = obs_ref[0, 128 * ah : 128 * ah + 128, 128 * t : 128 * t + 128]
            cols = lax.dot_general(pick, quarter, NT, preferred_element_type=F32)
            rows[pl.ds(2 * t + ah, 128, stride=8), :] = cols
    out_ref[...] = seen[...][:, 0:4].astype(BF16)
    for move in moves:
        move.wait()


def columns_ahead(rx_ref, seen_ref, tab_ref, out_ref):
    k2 = lax.broadcasted_iota(jnp.int32, (8, 512), 0)
    twist_c, twist_s = cos_sin(k2 * lax.broadcasted_iota(jnp.int32, (8, 512), 1))
    x = [rx_ref[j].astype(F32) for j in range(8)]
    e = [x[i] + x[i + 4] for i in range(4)]
    o = [x[i] - x[i + 4] for i in range(4)]
    up, down = (o[1] + o[3]) * HALF, (o[1] - o[3]) * HALF
    e02, e13 = e[0] + e[2], e[1] + e[3]
    d1 = (o[0] + down, o[2] + up)
    d2 = (e[0] - e[2], e[1] - e[3])
    d3 = (o[0] - down, up - o[2])
    spec = [(e02 + e13, None), d1, d2, d3, (e02 - e13, None), (d3[0], -d3[1]), (d2[0], -d2[1]), (d1[0], -d1[1])]
    rows = []
    for k2 in range(8):
        c, s = twist_c[k2 : k2 + 1], twist_s[k2 : k2 + 1]
        re, im = spec[k2]
        if im is None:
            zr, zi = re * c, re * s
        else:
            zr, zi = re * c - im * s, re * s + im * c
        rows.append(jnp.concatenate([zr, zi], axis=1))
    left = jnp.concatenate(rows, axis=0).astype(BF16)
    freq = jnp.dot(left, tab_ref[...], preferred_element_type=F32)

    out_ref[:, 2] = seen_ref[...]
    group = lane_group(64)
    for qg in range(4):
        part = freq[:, 128 * qg : 128 * qg + 128].reshape(8, 4, 8, 128)
        tiles = swap_groups([part[:, rg].reshape(64, 128) for rg in range(4)], group)
        for q4 in range(4):
            at = 8 * (4 * qg + q4)
            tile = tiles[q4].reshape(8, 8, 128).astype(BF16)
            out_ref[at : at + 8, 0] = tile[:, 0:4]
            out_ref[at : at + 8, 1] = tile[:, 4:8]


def rows_kernel(
    rx_ref, ct_ref, st_ref, cg_ref, sg_ref, tc_ref, ts_ref, chosen_ref, bits_ref, big_hbm,
    out_ref, ybuf, held, obs, rr, ct, st, cg, sg, keep, zbuf, tab_ref, sem,
):
    fetch = pltpu.make_async_copy(big_hbm.at[pl.ds(0, 2 * N)], tab_ref, sem)
    fetch.start()
    ct[...], st[...], cg[...], sg[...] = ct_ref[...], st_ref[...], cg_ref[...], sg_ref[...]
    group = lax.broadcasted_iota(jnp.int32, (8, 8, 128), 2) >> 5
    got = rx_ref[...].astype(F32)
    held[:, 0:4] = got[:, 0]
    held[:, 4:8] = got[:, 1]
    obs[:, 0:4] = got[:, 2]
    chosen = chosen_ref[...].astype(BF16)
    turn_c, turn_s = tc_ref[:8][None], ts_ref[:8][None]
    turn_ct = jnp.transpose(jnp.broadcast_to(tc_ref[:1], (256, 128)))
    turn_st = jnp.transpose(jnp.broadcast_to(ts_ref[:1], (256, 128)))

    @pl.loop(0, 16, unroll=UNROLL)
    def _(f):
        tile = held[pl.ds(8 * f, 8)]
        spread = jnp.stack([jnp.where(group == rg, tile, 0.0) for rg in range(4)], axis=1)
        right = spread.reshape(256, 128).astype(BF16)
        cols = lax.dot_general(chosen, right, NT, preferred_element_type=F32)
        at = pl.multiple_of(f * 256, 256)
        c, s = ct[...], st[...]
        for t in range(2):
            half = cols[128 * t : 128 * t + 128].astype(BF16)
            ybuf[128 * t : 128 * t + 128, pl.ds(2 * at, 256)] = half * c.astype(BF16)
            ybuf[128 * t : 128 * t + 128, pl.ds(2 * at + 256, 256)] = half * s.astype(BF16)
        ct[...], st[...] = spin(c, s, turn_ct, turn_st)
        named = (lax.shift_right_logical(bits_ref[...], f) & 1) == 1
        for t in range(2):
            kept = jnp.where(named, chosen_ref[128 * t : 128 * t + 128], 0.0)
            keep[pl.ds(at + 128 * t, 128)] = kept.astype(BF16)

    fetch.wait()
    pred = jnp.dot(ybuf[...], tab_ref[...], preferred_element_type=F32) * (1.0 / 64.0)
    seen, back = obs.reshape(1024, 128), rr.reshape(1024, 128)
    resid = []
    for t in range(2):
        halves = []
        for ah in range(2):
            guess = pred[128 * t : 128 * t + 128, 128 * ah : 128 * ah + 128]
            quarter = seen[pl.ds(2 * t + ah, 128, stride=8), :] - guess
            halves.append(jnp.transpose(quarter))
            back[pl.ds(2 * t + ah, 128, stride=8), :] = quarter
        resid.append(jnp.concatenate(halves, axis=0))
    resid = jnp.concatenate(resid, axis=1).astype(BF16)

    @pl.loop(0, 16, unroll=UNROLL1)
    def _(f):
        at = pl.multiple_of(f * 256, 256)
        both = jnp.dot(tab_ref[pl.ds(2 * at, 512), :], resid, preferred_element_type=F32)
        c, s = cg[...], sg[...]
        z = [c * both[:256, 128 * t : 128 * t + 128] + s * both[256:, 128 * t : 128 * t + 128] for t in range(2)]
        zbuf[pl.ds(at, 256)] = jnp.concatenate(z, axis=1).astype(BF16)
        nc, ns = spin(c.reshape(32, 8, 128), s.reshape(32, 8, 128), turn_c, turn_s)
        cg[...], sg[...] = nc.reshape(256, 128), ns.reshape(256, 128)

    @pl.loop(0, 16, unroll=UNROLL2)
    def _(f):
        at = pl.multiple_of(f * 256, 256)
        grid = jnp.dot(zbuf[pl.ds(at, 256)], keep[pl.ds(at, 256)], preferred_element_type=F32).reshape(8, 4, 8, 128)
        mixed = jnp.where(
            group < 2,
            jnp.where(group == 0, grid[:, 0], grid[:, 1]),
            jnp.where(group == 2, grid[:, 2], grid[:, 3]),
        )
        mixed = (mixed * (1.0 / 16.0)).astype(BF16)
        out_ref[pl.ds(8 * f, 8), 0] = mixed[:, 0:4]
        out_ref[pl.ds(8 * f, 8), 1] = mixed[:, 4:8]
        out_ref[pl.ds(8 * f, 8), 2] = rr[pl.ds(8 * f, 8)][:, 0:4].astype(BF16)


def columns_back(rx_ref, off_ref, tw_ref, tab_ref, img_ref, res_hbm, held, sent, res_ref, sem):
    got = rx_ref[...].astype(F32)
    held[:, 0:4] = got[:, 0]
    held[:, 4:8] = got[:, 1]
    u = own_column(off_ref)
    sent[:, 0:4] = got[:, 2]
    rows = sent.reshape(1024, 128)
    pick = selector(u)
    for t in range(2):
        for ah in range(2):
            quarter = jnp.transpose(rows[pl.ds(2 * t + ah, 128, stride=8), :]).astype(BF16)
            quarter = jnp.dot(quarter, pick, preferred_element_type=F32).astype(BF16)
            res_ref[0, 128 * ah : 128 * ah + 128, 128 * t : 128 * t + 128] = quarter
    leave = pltpu.make_async_copy(res_ref, res_hbm, sem)
    leave.start()
    tiles = held[...].reshape(16, 64, 128)
    group = lane_group(64)
    wide = [[None] * 4 for _ in range(4)]
    for qg in range(4):
        mixed = swap_groups([tiles[4 * qg + q4] for q4 in range(4)], group)
        for rg in range(4):
            wide[rg][qg] = mixed[rg].reshape(8, 8, 128)
    left = jnp.stack([jnp.concatenate(wide[rg], axis=2) for rg in range(4)], axis=1)
    left = left.reshape(256, 512).astype(BF16)
    both = jnp.dot(left, tab_ref[...], preferred_element_type=F32).reshape(8, 32, 1024)
    re, im = [], []
    for k2 in range(8):
        c, s = tw_ref[k2 : k2 + 1, :], tw_ref[8 + k2 : 9 + k2, :]
        a, b = spin(both[k2, :, :512], both[k2, :, 512:], c + s, s - c)
        re.append(a)
        im.append(b)
    a1, a2, a3 = re[1] + re[7], re[2] + re[6], re[3] + re[5]
    b1, b2, b3 = im[1] - im[7], im[2] - im[6], im[3] - im[5]
    plus, minus = re[0] + re[4], re[0] - re[4]
    even = [plus + a2, minus - b2, plus - a2, minus + b2]
    odd = [a1 + a3, HALF * (a1 - b1 - a3 - b3), b3 - b1, HALF * (a3 - a1 - b1 - b3)]
    for j in range(4):
        img_ref[j] = (even[j] + odd[j]).astype(BF16)
        img_ref[j + 4] = (even[j] - odd[j]).astype(BF16)
    leave.wait()


VMEM = pl.BlockSpec(memory_space=pltpu.VMEM)
HBM = pl.BlockSpec(memory_space=pltpu.HBM)
UNROLL, UNROLL1, UNROLL2 = 8, 8, 16
L0, L1, L2 = 56, 50, 52


def params(mebibytes):
    return pltpu.CompilerParams(vmem_limit_bytes=mebibytes * 2**20)


def on_device(sky_image, observed, offsets, assignments):
    ahead, back, twiddle = column_tables()
    big = jnp.asarray(np.concatenate([row_table(), ahead[:, :256], ahead[:, 256:]], axis=0))
    everyone = ("facet", "vis")
    message = jax.ShapeDtypeStruct((128, 3, 4, 128), BF16)
    offsets, assignments = offsets.T, assignments.T

    strips = pl.pallas_call(
        round_image,
        out_shape=jax.ShapeDtypeStruct((8, 32, 512), BF16),
        in_specs=[HBM],
        out_specs=HBM,
        scratch_shapes=[pltpu.VMEM((256, 512), F32), pltpu.VMEM((8, 32, 512), BF16), pltpu.SemaphoreType.DMA((8,))],
        compiler_params=params(L0),
    )(sky_image)
    strips = lax.all_to_all(strips, "vis", 0, 0, tiled=True)
    plan_shapes = [(128, 256), (128, 256), (256, 128), (256, 128), (16, 128), (16, 128), (256, 128)]
    seen, ahead_table, *plan = pl.pallas_call(
        observed_columns,
        out_shape=(
            jax.ShapeDtypeStruct((128, 4, 128), BF16),
            jax.ShapeDtypeStruct((1024, 512), BF16),
            *[jax.ShapeDtypeStruct(shape, F32) for shape in plan_shapes],
            jax.ShapeDtypeStruct((128, 128), jnp.int32),
        ),
        in_specs=[VMEM, VMEM, VMEM, HBM],
        out_specs=(VMEM,) * 10,
        scratch_shapes=[pltpu.VMEM((128, 8, 128), F32), pltpu.SemaphoreType.DMA((2,))],
        compiler_params=params(L1),
        cost_estimate=pl.CostEstimate(flops=10**9, bytes_accessed=4 * 10**6, transcendentals=0),
    )(observed, offsets, assignments, big)
    sent = pl.pallas_call(
        columns_ahead,
        out_shape=message,
        in_specs=[VMEM, VMEM, VMEM],
        out_specs=VMEM,
        compiler_params=params(32),
    )(strips, seen, ahead_table)
    got = lax.all_to_all(sent, everyone, 0, 0, tiled=True)
    sent = pl.pallas_call(
        rows_kernel,
        out_shape=message,
        in_specs=[VMEM] * 9 + [HBM],
        out_specs=VMEM,
        scratch_shapes=[
            pltpu.VMEM((256, 2 * N), BF16),
            pltpu.VMEM((128, 8, 128), F32),
            pltpu.VMEM((128, 8, 128), F32),
            pltpu.VMEM((128, 8, 128), F32),
            pltpu.VMEM((128, 256), F32),
            pltpu.VMEM((128, 256), F32),
            pltpu.VMEM((256, 128), F32),
            pltpu.VMEM((256, 128), F32),
            pltpu.VMEM((N, 128), BF16),
            pltpu.VMEM((N, 256), BF16),
            pltpu.VMEM((2 * N, 256), BF16),
            pltpu.SemaphoreType.DMA,
        ],
        compiler_params=params(L2),
    )(got, *plan, big)
    got = lax.all_to_all(sent, everyone, 0, 0, tiled=True)
    image, resid = pl.pallas_call(
        columns_back,
        out_shape=(
            jax.ShapeDtypeStruct((8, 32, 512), BF16),
            jax.ShapeDtypeStruct((1, SUB, SUB), BF16),
        ),
        in_specs=[VMEM, VMEM, VMEM, VMEM],
        out_specs=(VMEM, HBM),
        scratch_shapes=[
            pltpu.VMEM((128, 8, 128), F32),
            pltpu.VMEM((128, 8, 128), F32),
            pltpu.VMEM((1, SUB, SUB), BF16),
            pltpu.SemaphoreType.DMA,
        ],
        compiler_params=params(16),
    )(got, offsets, jnp.asarray(twiddle), jnp.asarray(back))
    image = lax.all_to_all(image, "vis", 0, 0, tiled=True)
    return resid, image.reshape(256, 512).astype(F32)


def solution(mesh):
    placed = (P("facet", "vis"), P(("facet", "vis"), None, None), P(), P())
    return jax.shard_map(
        on_device,
        mesh=mesh,
        in_specs=placed,
        out_specs=(P(("facet", "vis"), None, None), P("facet", "vis")),
        check_vma=False,
    )
```
